32 devices in a mesh: len: 4 (over z), wid: 4 (over y, x), lay: 2 (over core).
Axes of the slice: x: 2, y: 2, z: 4, core: 2. Of those that a mesh axis runs over, the one named last changes fastest.
Arguments:
- displacement: float32 [3, 16, 32, 256], P(None, 'len', 'wid', 'lay'), may hold values from -0.1 to 0.1
- velocity: float32 [3, 16, 32, 256], P(None, 'len', 'wid', 'lay'), may hold values from -1.5 to 1.5
- lame_first: float32 [16, 32, 256], P('len', 'wid', 'lay'), may hold values from 0.5 to 2
- shear_modulus: float32 [16, 32, 256], P('len', 'wid', 'lay'), may hold values from 0.5 to 2
- nodal_mass: float32 [16, 32, 256], P('len', 'wid', 'lay'), may hold values from 1 to 4
- slave_nodes: int32 [4, 4, 2, 64, 128], P('len', 'wid', 'lay'), may hold values from 0 to 4095
- initial_gap: float32 [4, 4, 2, 64, 128], P('len', 'wid', 'lay'), may hold values from -0.15 to 0.1
- candidate: int32 [4, 4, 2, 64, 128], P('len', 'wid', 'lay'), may hold values from 0 to 127
- pair_owner: int32 [4, 4, 2, 64, 1], P('len', 'wid', 'lay'), may hold values from 0 to 15; in each aligned block of 64 rows (0 to 63, 64 to 127, ..., all dimensions but the last counted through in order) at most 8 rows name the same one
- pair_patch: int32 [4, 4, 2, 64], P('len', 'wid', 'lay'), may hold values from 0 to 31
- master_faces: int32 [4, 4, 2, 32, 128], P('len', 'wid', 'lay'), may hold values from 0 to 2943, as said below
Outputs:
- new_displacement: float32 [3, 16, 32, 256], P(None, 'len', 'wid', 'lay')
- new_velocity: float32 [3, 16, 32, 256], P(None, 'len', 'wid', 'lay')
The draws below stay inside these ranges and needn't reach their ends.
Inputs may be any that keep to these rules, and one draw needn't show every extreme that they name: `slave_nodes`: local node numbers of the device's own block. `candidate`: a face's position within the pair's master patch. `pair_owner`: owners are numbered len index * 4 + wid index and share the device's lay index; among the rows of one device no owner is named more than 8 times, a bound that some block reaches. `pair_patch`: a master patch of the owner. `master_faces`: a face's first node is i * 8 * 128 + j * 128 + k with i < 3 and j < 7, so all 4 of its nodes lie on the owner.
All inputs are finite; a program needn't handle non-finite values.
Results may differ from the reference program's by a relative error of at most 0.00005.
Values sent between devices are 32-bit elements; how exact they have to be, the bound alone decides.
A program may use at most 64 MiB of HBM per device.

```python
import math
import jax
import jax.numpy as jnp
import numpy as np

CX = 4
CY = 8
CZ = 128
PAIRS = 64
PATCH = 128
MPATCH = 32
STEPS = 2
NX = 16
NY = 32
NZ = 256
CAP = 8
N_LEN = 4
N_WID = 4
N_LAY = 2


def draw_master_faces(key, part):
    shape = (NX // CX, NY // CY, NZ // CZ, MPATCH, PATCH)
    key_x, key_y, key_z = jax.random.split(jax.random.fold_in(key, 17), 3)
    row_x = jax.random.randint(key_x, shape, 0, CX - 1)
    row_y = jax.random.randint(key_y, shape, 0, CY - 1)
    row_z = jax.random.randint(key_z, shape, 0, CZ)
    faces = ((row_x * CY + row_y) * CZ + row_z).astype(jnp.int32)
    highest = ((CX - 2) * CY + CY - 2) * CZ + CZ - 1
    return faces.at[:, :, :, 0, 0].set(highest).astype(jnp.int32)


def set_ends(values, rng, smallest, top_value):
    dims = values.shape
    spot = [jax.random.randint(jax.random.fold_in(rng, axis), (), 0, dims[axis]) for axis in range(len(dims))]
    values = values.at[tuple(spot)].set(smallest)
    longest = dims.index(max(dims))
    spot[longest] = (spot[longest] + 1) % dims[longest]
    return values.at[tuple(spot)].set(top_value)


def levels(stream_key, shape, cuts, least, high):
    gain, own = 1.0, jax.random.fold_in(stream_key, 6)
    for axis_at, blocks in cuts:
        draws = jnp.exp(jax.random.uniform(jax.random.fold_in(own, axis_at), (blocks,), jnp.float32, least / len(cuts), high / len(cuts)))
        gain = gain * jnp.repeat(draws, shape[axis_at] // blocks).reshape([-1 if axis == axis_at else 1 for axis in range(len(shape))])
    return gain


def routed_block(stream_key, own, number, rows, amount, top, reach, skew):
    order = jax.random.permutation(stream_key, amount)
    heavy_load, common = portions_of(amount, rows * top, reach, skew, True), portions_of(amount, rows * top, reach, skew, False)
    places = jnp.arange(amount)

    def named(sizes, offset_by):
        used = int((sizes > 0).sum())
        fixed = max(1, used // 4)
        moved = fixed + (places - fixed + offset_by * (used - fixed)) % max(1, amount - fixed)
        return jnp.zeros((amount,), jnp.int32).at[order[jnp.where(places < fixed, places, moved)]].set(jnp.asarray(sizes, jnp.int32))

    sizes = jnp.where(number % 4 == 0, named(heavy_load, number // 4), named(common, number - number // 4 - 1))
    mixed = jax.random.permutation(jax.random.fold_in(own, 3), amount)
    giver, sink = mixed[0:amount // 2 * 2:2], mixed[1:amount // 2 * 2:2]
    slack = jnp.minimum(sizes[giver] - 1, reach - sizes[sink]) // 2
    slack = jnp.where((giver == order[0]) | (sink == order[0]) | (sizes[sink] == 0), 0, jnp.maximum(slack, 0))
    moved = jax.random.randint(jax.random.fold_in(own, 4), (amount // 2,), 0, 1 << 20) % (slack + 1)
    sizes = sizes.at[giver].add(-moved).at[sink].add(moved)
    items = jnp.searchsorted(jnp.cumsum(sizes), jnp.arange(rows * top), side="right").astype(jnp.int32)
    table = items.reshape(top, rows).T
    table = table[jax.random.permutation(jax.random.fold_in(own, 1), rows)]
    offset_by = jax.random.randint(jax.random.fold_in(own, 2), (rows, 1), 0, top)
    return jnp.take_along_axis(table, (jnp.arange(top)[None, :] + offset_by) % top, axis=1)


def portions_of(number_of, total, reach, skew, full):
    loads = [(1 << 20) // math.isqrt(standing ** skew) + 1 for standing in range(1, number_of + 1)]
    largest = reach if full else min(reach, max(-(-total // number_of), total * loads[0] // sum(loads)))
    least = 1 if total - largest >= number_of - 1 else 0
    given, spare = [largest] + [least] * (number_of - 1), total - largest - least * (number_of - 1)
    while spare > 0:
        candidates = [i for i in range(1, number_of) if given[i] < largest] or [i for i in range(1, number_of) if given[i] < reach]
        mass, budget = sum([loads[i] for i in candidates]), spare
        for i in candidates:
            more = min(reach - given[i], max(1, budget * loads[i] // mass), spare)
            given[i] = given[i] + more
            spare = spare - more
    return np.array(given)


def noise(stream_key, dims, width, reach, pieces=(), kind=jnp.bfloat16):
    loudness = levels(stream_key, dims, pieces, -0.22, 0.18) if pieces else 1.0
    entries = jax.random.normal(stream_key, dims, jnp.float32) * width * loudness
    return jnp.minimum(jnp.maximum(entries, -reach), reach).astype(kind)


def setup_inputs(seed: int = 0) -> dict:
    splits = jax.random.split(jax.random.key(seed), 12)
    displacement = jnp.clip(jax.random.uniform(splits[0], (3, NX, NY, NZ), jnp.float32, -0.1, 0.1) * levels(splits[0], (3, NX, NY, NZ), ((1, 4), (2, 4), (3, 2)), -0.4, 0.0), -0.1, 0.1)
    velocity = noise(splits[1], (3, NX, NY, NZ), 0.3, 1.5, ((1, 4), (2, 4), (3, 2)), jnp.float32)
    lame_first = jnp.clip(jnp.exp(math.log(2.0) - 1.3862944 * jax.random.uniform(splits[2], (NX, NY, NZ), jnp.float32) ** levels(splits[2], (NX, NY, NZ), ((0, 4), (1, 4), (2, 2)), -0.2, 0.2)), 0.5, 2.0)
    shear_modulus = jnp.clip(jnp.exp(math.log(2.0) - 1.3862944 * jax.random.uniform(splits[3], (NX, NY, NZ), jnp.float32) ** levels(splits[3], (NX, NY, NZ), ((0, 4), (1, 4), (2, 2)), -0.2, 0.2)), 0.5, 2.0)
    nodal_mass = jnp.clip(jnp.exp(math.log(4.0) - 1.3862944 * jax.random.uniform(splits[4], (NX, NY, NZ), jnp.float32) ** levels(splits[4], (NX, NY, NZ), ((0, 4), (1, 4), (2, 2)), -0.2, 0.2)), 1.0, 4.0)
    slave_nodes = set_ends(jax.random.randint(splits[5], (N_LEN, N_WID, N_LAY, PAIRS, PATCH), 0, CX * CY * CZ), jax.random.fold_in(splits[5], 1), 0, (CX * CY * CZ) - 1).astype(jnp.int32)
    initial_gap = jnp.clip(-0.15 + 0.25 * jax.random.uniform(splits[6], (N_LEN, N_WID, N_LAY, PAIRS, PATCH), jnp.float32) ** levels(splits[6], (N_LEN, N_WID, N_LAY, PAIRS, PATCH), ((0, 4), (1, 4), (2, 2)), -0.2, 0.2), -0.15, 0.1)
    candidate = set_ends(jax.random.randint(splits[7], (N_LEN, N_WID, N_LAY, PAIRS, PATCH), 0, PATCH), jax.random.fold_in(splits[7], 1), 0, PATCH - 1).astype(jnp.int32)
    pair_owner_keys = jax.random.split(jax.random.fold_in(splits[8], 1), N_LEN * N_WID * N_LAY * PAIRS // PAIRS)
    pair_owner_turns = jax.random.permutation(jax.random.fold_in(splits[8], 3), N_LEN * N_WID * N_LAY * PAIRS // PAIRS)
    pair_owner = jax.vmap(lambda own, number: routed_block(jax.random.fold_in(splits[8], 2), own, number, PAIRS, N_LEN * N_WID, 1, CAP, 2))(pair_owner_keys, pair_owner_turns).reshape((N_LEN, N_WID, N_LAY, PAIRS, 1))
    pair_patch = set_ends(jax.random.randint(splits[9], (N_LEN, N_WID, N_LAY, PAIRS), 0, MPATCH), jax.random.fold_in(splits[9], 1), 0, MPATCH - 1).astype(jnp.int32)
    master_faces = draw_master_faces(jax.random.fold_in(splits[11], 71), 0)
    return {"displacement": displacement, "velocity": velocity, "lame_first": lame_first, "shear_modulus": shear_modulus, "nodal_mass": nodal_mass, "slave_nodes": slave_nodes, "initial_gap": initial_gap, "candidate": candidate, "pair_owner": pair_owner, "pair_patch": pair_patch, "master_faces": master_faces}


penalty = 4.0
hourglass = 0.3
time_step = 0.25
corner_offsets = ((0, 0, 0), (1, 0, 0), (0, 1, 0), (1, 1, 0), (0, 0, 1), (1, 0, 1), (0, 1, 1), (1, 1, 1))

def element_mean(values, counts):
    summed = jnp.zeros(counts, jnp.float32)
    for along_x, along_y, along_z in corner_offsets:
        summed = summed + values[along_x:along_x + counts[0], along_y:along_y + counts[1], along_z:along_z + counts[2]]
    return summed * 0.125

def corner_forces(points, lame_elem, shear_elem, counts):
    corners = []
    for along_x, along_y, along_z in corner_offsets:
        corners.append(points[:, along_x:along_x + counts[0], along_y:along_y + counts[1], along_z:along_z + counts[2]])
    mean_disp = corners[0]
    for corner in corners[1:]:
        mean_disp = mean_disp + corner
    mean_disp = mean_disp * 0.125
    columns = []
    for axis_pos in range(3):
        column = jnp.zeros_like(corners[0])
        for offsets, corner in zip(corner_offsets, corners):
            column = column + (2 * offsets[axis_pos] - 1) * corner
        columns.append(column * 0.25)
    gradient = jnp.stack(columns, axis=1)
    strain_trace = gradient[0, 0] + gradient[1, 1] + gradient[2, 2]
    stress = shear_elem * (gradient + jnp.swapaxes(gradient, 0, 1))
    stress = stress + lame_elem * strain_trace * jnp.eye(3, dtype=jnp.float32)[:, :, None, None, None]
    damping = hourglass * shear_elem
    forces = []
    for offsets, corner in zip(corner_offsets, corners):
        unit_signs = [2 * offsets[0] - 1, 2 * offsets[1] - 1, 2 * offsets[2] - 1]
        traction = unit_signs[0] * stress[:, 0] + unit_signs[1] * stress[:, 1] + unit_signs[2] * stress[:, 2]
        linear = unit_signs[0] * gradient[:, 0] + unit_signs[1] * gradient[:, 1] + unit_signs[2] * gradient[:, 2]
        forces.append(-0.25 * traction - damping * (corner - mean_disp - 0.5 * linear))
    return forces

def face_frame(u_flat, node_one, node_two, node_three, node_four):
    at_one = u_flat[:, node_one]
    at_two = u_flat[:, node_two]
    at_three = u_flat[:, node_three]
    at_four = u_flat[:, node_four]
    centroid = (at_one + at_two + at_three + at_four) * 0.25
    shape_tail = (3,) + (1,) * node_one.ndim
    diag_one = at_three - at_one + jnp.array([1.0, 1.0, 0.0], dtype=jnp.float32).reshape(shape_tail)
    diag_two = at_four - at_two + jnp.array([-1.0, 1.0, 0.0], dtype=jnp.float32).reshape(shape_tail)
    normal = jnp.stack([diag_one[1] * diag_two[2] - diag_one[2] * diag_two[1], diag_one[2] * diag_two[0] - diag_one[0] * diag_two[2], diag_one[0] * diag_two[1] - diag_one[1] * diag_two[0]])
    normal = normal / jnp.sqrt(normal[0] * normal[0] + normal[1] * normal[1] + normal[2] * normal[2])
    return (centroid, normal)

def contact_terms(centroid, normal, slave_disp, gap_start):
    gap_now = gap_start + (slave_disp[0] - centroid[0]) * normal[0] + (slave_disp[1] - centroid[1]) * normal[1] + (slave_disp[2] - centroid[2]) * normal[2]
    penetration = jnp.minimum(gap_now, 0.0)
    return -penalty * penetration * normal

def to_global(local, dev_len, dev_wid, dev_lay):
    index_x = local // (CY * CZ)
    index_y = local // CZ % CY
    index_z = local % CZ
    return ((dev_len * CX + index_x) * NY + (dev_wid * CY + index_y)) * NZ + (dev_lay * CZ + index_z)

def reference(displacement, velocity, lame_first, shear_modulus, nodal_mass, slave_nodes, initial_gap, candidate, pair_owner, pair_patch, master_faces):
    counts = (NX - 1, NY - 1, NZ - 1)
    lame_elem = element_mean(lame_first, counts)
    shear_elem = element_mean(shear_modulus, counts)
    dev_len = jnp.arange(N_LEN, dtype=jnp.int32)[:, None, None, None, None]
    dev_wid = jnp.arange(N_WID, dtype=jnp.int32)[None, :, None, None, None]
    dev_lay = jnp.arange(N_LAY, dtype=jnp.int32)[None, None, :, None, None]
    slaves_global = to_global(slave_nodes, dev_len, dev_wid, dev_lay)
    owners = pair_owner[..., 0]
    own_len = (owners // N_WID)[..., None]
    own_wid = (owners % N_WID)[..., None]
    face_local = master_faces[own_len, own_wid, dev_lay, pair_patch[..., None], candidate]
    node_one = to_global(face_local, own_len, own_wid, dev_lay)
    node_two = node_one + NY * NZ
    node_three = node_one + NY * NZ + NZ
    node_four = node_one + NZ
    for step in range(STEPS):
        forces = corner_forces(displacement, lame_elem, shear_elem, counts)
        internal = jnp.zeros((3, NX, NY, NZ), jnp.float32)
        for offsets, force in zip(corner_offsets, forces):
            padded = jnp.pad(force, ((0, 0), (1, 1), (1, 1), (1, 1)))
            internal = internal + padded[:, 1 - offsets[0]:1 - offsets[0] + NX, 1 - offsets[1]:1 - offsets[1] + NY, 1 - offsets[2]:1 - offsets[2] + NZ]
        u_flat = displacement.reshape(3, -1)
        centroid, normal = face_frame(u_flat, node_one, node_two, node_three, node_four)
        slave_force = contact_terms(centroid, normal, u_flat[:, slaves_global], initial_gap)
        contact = jnp.zeros((3, NX * NY * NZ), jnp.float32).at[:, slaves_global].add(slave_force)
        quarter = -0.25 * slave_force
        contact = contact.at[:, node_one].add(quarter)
        contact = contact.at[:, node_two].add(quarter)
        contact = contact.at[:, node_three].add(quarter)
        contact = contact.at[:, node_four].add(quarter)
        total_force = internal + contact.reshape(3, NX, NY, NZ)
        velocity = velocity + time_step * total_force / nodal_mass[None]
        displacement = displacement + time_step * velocity
    return (displacement, velocity)
```

```python
import functools

import jax
import jax.numpy as jnp
from jax import lax
from jax.experimental import pallas as pl
from jax.experimental.pallas import tpu as pltpu
from jax.sharding import PartitionSpec as P

STEPS = 2


penalty = 4.0
hourglass = 0.3
time_step = 0.25
corner_offsets = (
    (0, 0, 0),
    (1, 0, 0),
    (0, 1, 0),
    (1, 1, 0),
    (0, 0, 1),
    (1, 0, 1),
    (0, 1, 1),
    (1, 1, 1),
)
f32 = jnp.float32
bf16 = jnp.bfloat16
CHUNK = 8


def padded_2(cells, sides, width):
    for axis, dim in sides:
        count = lax.axis_size(axis)
        ends = count - 1
        head = lax.slice_in_dim(cells, 0, width, axis=dim)
        tail = lax.slice_in_dim(cells, cells.shape[dim] - width, cells.shape[dim], axis=dim)
        cells = jnp.concatenate(
            [
                lax.ppermute(tail, axis, [(i, (i + 1) % count) for i in range(ends)]),
                cells,
                lax.ppermute(head, axis, [((i + 1) % count, i) for i in range(ends)]),
            ],
            axis=dim,
        )
    return cells


def element_mean(values, counts):
    summed = jnp.zeros(counts, jnp.float32)
    for along_x, along_y, along_z in corner_offsets:
        summed = (
            summed
            + values[
                along_x : along_x + counts[0],
                along_y : along_y + counts[1],
                along_z : along_z + counts[2],
            ]
        )
    return summed * 0.125


def corner_forces(points, lame_elem, shear_elem, counts):
    corners = []
    for along_x, along_y, along_z in corner_offsets:
        corners.append(
            points[
                :,
                along_x : along_x + counts[0],
                along_y : along_y + counts[1],
                along_z : along_z + counts[2],
            ]
        )
    mean_disp = corners[0]
    for corner in corners[1:]:
        mean_disp = mean_disp + corner
    mean_disp = mean_disp * 0.125
    columns = []
    for axis_pos in range(3):
        column = jnp.zeros_like(corners[0])
        for offsets, corner in zip(corner_offsets, corners):
            column = column + (2 * offsets[axis_pos] - 1) * corner
        columns.append(column * 0.25)
    gradient = jnp.stack(columns, axis=1)
    strain_trace = gradient[0, 0] + gradient[1, 1] + gradient[2, 2]
    stress = shear_elem * (gradient + jnp.swapaxes(gradient, 0, 1))
    stress = (
        stress + lame_elem * strain_trace * jnp.eye(3, dtype=jnp.float32)[:, :, None, None, None]
    )
    damping = hourglass * shear_elem
    forces = []
    for offsets, corner in zip(corner_offsets, corners):
        unit_signs = [2 * offsets[0] - 1, 2 * offsets[1] - 1, 2 * offsets[2] - 1]
        traction = (
            unit_signs[0] * stress[:, 0]
            + unit_signs[1] * stress[:, 1]
            + unit_signs[2] * stress[:, 2]
        )
        linear = (
            unit_signs[0] * gradient[:, 0]
            + unit_signs[1] * gradient[:, 1]
            + unit_signs[2] * gradient[:, 2]
        )
        forces.append(-0.25 * traction - damping * (corner - mean_disp - 0.5 * linear))
    return forces


def valid_rows(length, position, pieces):
    element_low = jnp.arange(length + 1, dtype=jnp.int32) + position * length - 1
    return ((element_low >= 0) & (element_low <= pieces * length - 2)).astype(jnp.float32)


def halves(x):
    high = x.astype(bf16)
    return high, (x - high.astype(f32)).astype(bf16)


def hot(rows, depth):
    n = rows[0].shape[1]
    iota = lax.broadcasted_iota(jnp.int32, (depth, n), 0)
    return jnp.concatenate(
        [jnp.where(iota == r, 1.0, 0.0).astype(bf16) for r in rows], axis=1
    )


def pick(table, idx, comps, tall):
    lanes = table.shape[1] // 2
    n = idx.shape[1]
    rows = [idx[j : j + 1, :] for j in range(CHUNK)]
    lane_hot = hot([r % lanes for r in rows], lanes)
    wide = jnp.dot(
        table, jnp.concatenate([lane_hot, lane_hot], axis=0), preferred_element_type=f32
    )
    iota = lax.broadcasted_iota(jnp.int32, (tall, n), 0)
    out = [[] for _ in range(comps)]
    for j in range(CHUNK):
        match = iota == jnp.where(rows[j] < 0, -1, rows[j] // lanes)
        for c in range(comps):
            block = wide[c * tall : (c + 1) * tall, j * n : (j + 1) * n]
            out[c].append(jnp.sum(jnp.where(match, block, 0.0), axis=0, keepdims=True))
    return [jnp.concatenate(o, axis=0) for o in out]


def spread(values, idx, tall, lanes):
    n = idx.shape[1]
    rows = [idx[j : j + 1, :] for j in range(CHUNK)]
    lane_hot = hot([r % lanes for r in rows], lanes)
    iota = lax.broadcasted_iota(jnp.int32, (tall, n), 0)
    match = [iota == jnp.where(r < 0, -1, r // lanes) for r in rows]
    blocks = []
    for v in values:
        for half in halves(v):
            half = half.astype(f32)
            blocks.append(
                jnp.concatenate(
                    [
                        jnp.where(match[j], half[j : j + 1, :], 0.0).astype(bf16)
                        for j in range(CHUNK)
                    ],
                    axis=1,
                )
            )
    return lax.dot_general(
        jnp.concatenate(blocks, axis=0),
        lane_hot,
        (((1,), (1,)), ((), ())),
        preferred_element_type=f32,
    )


def joined(halved, comps, tall):
    return [
        halved[2 * c * tall : (2 * c + 1) * tall] + halved[(2 * c + 1) * tall : (2 * c + 2) * tall]
        for c in range(comps)
    ]


def as_table(blocks):
    both = [halves(b) for b in blocks]
    return jnp.concatenate(
        [
            jnp.concatenate([b[0] for b in both], axis=0),
            jnp.concatenate([b[1] for b in both], axis=0),
        ],
        axis=1,
    )


def exact_dot(a, b):
    return jnp.dot(a, b, precision=lax.Precision.HIGHEST, preferred_element_type=f32)


def flat_block(u, c):
    return jnp.concatenate([u[c, i] for i in range(u.shape[1])], axis=0)


def slave_disp_rows(u_ref, slaves_ref, out_ref):
    u = u_ref[...]
    tall = u.shape[1] * u.shape[2]
    table = as_table([flat_block(u, c) for c in range(3)])

    def body(t, _):
        at = pl.ds(pl.multiple_of(t * CHUNK, CHUNK), CHUNK)
        got = pick(table, slaves_ref[at, :], 3, tall)
        for c in range(3):
            out_ref[c, at, :] = got[c]
        return 0

    lax.fori_loop(0, slaves_ref.shape[0] // CHUNK, body, 0)


def slot_matrix(col, row, capacity, slots):
    pairs = row.shape[1]
    earlier = lax.broadcasted_iota(jnp.int32, (pairs, pairs), 0) < lax.broadcasted_iota(
        jnp.int32, (pairs, pairs), 1
    )
    rank = jnp.sum(jnp.where((col == row) & earlier, 1.0, 0.0), axis=0, keepdims=True)
    slot = row * capacity + rank.astype(jnp.int32)
    return jnp.where(
        lax.broadcasted_iota(jnp.int32, (slots, pairs), 0) == slot, 1.0, 0.0
    ).astype(f32)


def to_groups(rows, groups):
    return rows.reshape(groups, rows.shape[0] // groups, rows.shape[1])


def first_send_kernel(
    capacity,
    u_ref, slaves_ref, gap_ref, chosen_ref, col_ref, row_ref, patch_ref, out_ref, slot_ref, rows_ref
):
    groups, _, chunk, n = out_ref.shape
    slots = groups * chunk
    slave_disp_rows(u_ref, slaves_ref, rows_ref)
    to_slot = slot_matrix(col_ref[...], row_ref[...], capacity, slots)
    slot_ref[...] = to_slot
    face_id = (patch_ref[...] * n + chosen_ref[...] + 1).astype(f32)
    for c in range(3):
        out_ref[:, c] = to_groups(exact_dot(to_slot, rows_ref[c]), groups)
    out_ref[:, 3] = to_groups(exact_dot(to_slot, gap_ref[...]), groups)
    out_ref[:, 4] = to_groups(exact_dot(to_slot, face_id) - 1.0, groups)


def next_send_kernel(u_ref, slaves_ref, slot_ref, out_ref, rows_ref):
    groups = out_ref.shape[0]
    slave_disp_rows(u_ref, slaves_ref, rows_ref)
    for c in range(3):
        out_ref[:, c] = to_groups(exact_dot(slot_ref[...], rows_ref[c]), groups)


def face_nodes_rows(static_ref, faces_ref, nodes_ref):
    faces = faces_ref[...]
    patches, n = faces.shape
    table = jnp.concatenate(
        [(faces // n).astype(f32).astype(bf16), (faces % n).astype(f32).astype(bf16)], axis=0
    )
    table = jnp.concatenate([table, jnp.zeros_like(table)], axis=1)

    def body(t, _):
        face_id = static_ref[t, static_ref.shape[1] - 1].astype(jnp.int32)
        high, low = pick(table, face_id, 2, patches)
        node = high.astype(jnp.int32) * n + low.astype(jnp.int32)
        nodes_ref[t] = jnp.where(face_id < 0, -1, node)
        return 0

    lax.fori_loop(0, static_ref.shape[0], body, 0)


def frames(u):
    span_x, span_y, lanes = u.shape[1:]
    iota_x = lax.broadcasted_iota(jnp.int32, (span_x, span_y, lanes), 0)
    iota_y = lax.broadcasted_iota(jnp.int32, (span_x, span_y, lanes), 1)
    valid = (iota_x < span_x - 1) & (iota_y < span_y - 1)

    def shift_x(v):
        return jnp.concatenate([v[1:], v[:1]], axis=0)

    def shift_y(v):
        return jnp.stack([pltpu.roll(v[i], span_y - 1, 0) for i in range(span_x)])

    one = [u[c] for c in range(3)]
    two = [shift_x(v) for v in one]
    four = [shift_y(v) for v in one]
    three = [shift_x(v) for v in four]
    centroid = [(one[c] + two[c] + three[c] + four[c]) * 0.25 for c in range(3)]
    a = [three[0] - one[0] + 1.0, three[1] - one[1] + 1.0, three[2] - one[2]]
    b = [four[0] - two[0] - 1.0, four[1] - two[1] + 1.0, four[2] - two[2]]
    normal = [
        a[1] * b[2] - a[2] * b[1],
        a[2] * b[0] - a[0] * b[2],
        a[0] * b[1] - a[1] * b[0],
    ]
    square = normal[0] * normal[0] + normal[1] * normal[1] + normal[2] * normal[2]
    usable = valid & (square > 0.0)
    scale = jnp.where(usable, 1.0 / jnp.sqrt(jnp.where(usable, square, 1.0)), 0.0)
    return centroid, [v * scale for v in normal]


def owner_rows(u_ref, recv_ref, gap_ref, gap_at, nodes_ref, force_ref, halved_ref):
    u = u_ref[...]
    span_x, span_y, lanes = u.shape[1:]
    tall = span_x * span_y
    centroid, normal = frames(u)
    table = as_table(
        [jnp.concatenate([v[i] for i in range(span_x)], axis=0) for v in centroid + normal]
    )
    halved_ref[...] = jnp.zeros_like(halved_ref)

    def body(t, _):
        idx = nodes_ref[t]
        got = pick(table, idx, 6, tall)
        gap = gap_ref[t, gap_at]
        for c in range(3):
            gap = gap + (recv_ref[t, c] - got[c]) * got[3 + c]
        push = -penalty * jnp.minimum(gap, 0.0)
        force = [push * got[3 + c] for c in range(3)]
        for c in range(3):
            force_ref[t, c] = force[c]
        halved_ref[...] += spread(force, idx, tall, lanes)
        return 0

    lax.fori_loop(0, recv_ref.shape[0], body, 0)
    total = joined(halved_ref[...], 3, tall)
    out = []
    zero = jnp.zeros((span_y, lanes), f32)
    for c in range(3):
        quarter = [-0.25 * total[c][i * span_y : (i + 1) * span_y] for i in range(span_x)]
        in_x = [(quarter[i] if i < span_x - 1 else zero) + (quarter[i - 1] if i else zero) for i in range(span_x)]
        out.append([v + pltpu.roll(v, 1, 0) for v in in_x])
    return out


def owner_first_kernel(u_ref, recv_ref, faces_ref, force_ref, out_ref, nodes_ref, halved_ref):
    face_nodes_rows(recv_ref, faces_ref, nodes_ref)
    out = owner_rows(u_ref, recv_ref, recv_ref, 3, nodes_ref, force_ref, halved_ref)
    for c in range(3):
        for i in range(len(out[c])):
            out_ref[c, i] = out[c][i]


def owner_next_kernel(u_ref, recv_ref, first_ref, nodes_ref, force_ref, out_ref, halved_ref):
    out = owner_rows(u_ref, recv_ref, first_ref, 3, nodes_ref, force_ref, halved_ref)
    for c in range(3):
        for i in range(len(out[c])):
            out_ref[c, i] = out[c][i]


def slave_kernel(recv_ref, slot_ref, slaves_ref, other_ref, out_ref, rows_ref, halved_ref):
    groups, _, capacity, n = recv_ref.shape
    span_x, span_y, lanes = out_ref.shape[1:]
    tall = span_x * span_y
    for c in range(3):
        rows_ref[c] = lax.dot_general(
            slot_ref[...],
            recv_ref[:, c].reshape(groups * capacity, n),
            (((0,), (0,)), ((), ())),
            precision=lax.Precision.HIGHEST,
            preferred_element_type=f32,
        )
    halved_ref[...] = jnp.zeros_like(halved_ref)

    def body(t, _):
        at = pl.ds(pl.multiple_of(t * CHUNK, CHUNK), CHUNK)
        halved_ref[...] += spread(
            [rows_ref[c, at, :] for c in range(3)], slaves_ref[at, :], tall, lanes
        )
        return 0

    lax.fori_loop(0, slaves_ref.shape[0] // CHUNK, body, 0)
    total = joined(halved_ref[...], 3, tall)
    for c in range(3):
        for i in range(span_x):
            out_ref[c, i] = other_ref[c, i] + total[c][i * span_y : (i + 1) * span_y]


def call(kernel, outs, scratch, *args):
    return pl.pallas_call(
        kernel,
        out_shape=[jax.ShapeDtypeStruct(s, d) for s, d in outs],
        in_specs=[pl.BlockSpec(memory_space=pltpu.VMEM)] * len(args),
        out_specs=[pl.BlockSpec(memory_space=pltpu.VMEM)] * len(outs),
        scratch_shapes=[pltpu.VMEM(s, f32) for s in scratch],
        compiler_params=pltpu.CompilerParams(vmem_limit_bytes=40 * 1024 * 1024),
    )(*args)


def exchange(buffer):
    return lax.all_to_all(buffer, ("len", "wid"), split_axis=0, concat_axis=0, tiled=True)


def per_device(
    displacement,
    velocity,
    lame_first,
    shear_modulus,
    nodal_mass,
    slave_nodes,
    initial_gap,
    candidate,
    pair_owner,
    pair_patch,
    master_faces,
):
    span_x, span_y, span_z = (displacement.shape[1], displacement.shape[2], displacement.shape[3])
    n_len = lax.axis_size("len")
    n_wid = lax.axis_size("wid")
    groups = n_len * n_wid
    pairs = slave_nodes.shape[3]
    face_count = slave_nodes.shape[4]
    patches = master_faces.shape[3]
    capacity = max(2, 2 * pairs // groups)
    slots = groups * capacity
    blocks = slots // CHUNK
    tall = span_x * span_y
    slaves = slave_nodes.reshape(pairs, face_count)
    gaps = initial_gap.reshape(pairs, face_count)
    chosen = candidate.reshape(pairs, face_count)
    faces = master_faces.reshape(patches, face_count)
    col = pair_owner.reshape(pairs, 1)
    row = pair_owner.reshape(1, pairs)
    patch = pair_patch.reshape(pairs, 1)
    stacked = jnp.stack([lame_first, shear_modulus])
    rim = padded_2(stacked, (("len", 1), ("wid", 2), ("lay", 3)), 1)
    counts = (span_x + 1, span_y + 1, span_z + 1)
    mask_x = valid_rows(span_x, lax.axis_index("len"), n_len)
    mask_y = valid_rows(span_y, lax.axis_index("wid"), n_wid)
    mask_z = valid_rows(span_z, lax.axis_index("lay"), lax.axis_size("lay"))
    mask_all = mask_x[:, None, None] * mask_y[None, :, None] * mask_z[None, None, :]
    lame_elem = element_mean(rim[0], counts) * mask_all
    shear_elem = element_mean(rim[1], counts) * mask_all
    block = (3, span_x, span_y, span_z)

    def to_blocks(x):
        comps = x.shape[1]
        if capacity == CHUNK:
            return x
        return (
            x.reshape(blocks, CHUNK // capacity, comps, capacity, face_count)
            .transpose(0, 2, 1, 3, 4)
            .reshape(blocks, comps, CHUNK, face_count)
        )

    def from_blocks(x):
        comps = x.shape[1]
        if capacity == CHUNK:
            return x
        return (
            x.reshape(blocks, comps, CHUNK // capacity, capacity, face_count)
            .transpose(0, 2, 1, 3, 4)
            .reshape(groups, comps, capacity, face_count)
        )

    for step in range(STEPS):
        if step == 0:
            sent, to_slot = call(
                functools.partial(first_send_kernel, capacity),
                [((blocks, 5, CHUNK, face_count), f32), ((slots, pairs), f32)],
                [(3, pairs, face_count)],
                displacement, slaves, gaps, chosen, col, row, patch,
            )
        else:
            (sent,) = call(
                next_send_kernel,
                [((blocks, 3, CHUNK, face_count), f32)],
                [(3, pairs, face_count)],
                displacement, slaves, to_slot,
            )
        arrived = to_blocks(exchange(from_blocks(sent)))
        padded = padded_2(displacement, (("len", 1), ("wid", 2), ("lay", 3)), 1)
        forces = corner_forces(padded, lame_elem, shear_elem, counts)
        internal = jnp.zeros((3, span_x, span_y, span_z), jnp.float32)
        for offsets, force in zip(corner_offsets, forces):
            internal = (
                internal
                + force[
                    :,
                    1 - offsets[0] : 1 - offsets[0] + span_x,
                    1 - offsets[1] : 1 - offsets[1] + span_y,
                    1 - offsets[2] : 1 - offsets[2] + span_z,
                ]
            )
        force_shape = ((blocks, 3, CHUNK, face_count), f32)
        halved = [(6 * tall, span_z)]
        if step == 0:
            first = arrived
            force, reaction, nodes = call(
                owner_first_kernel,
                [force_shape, (block, f32), ((blocks, CHUNK, face_count), jnp.int32)],
                halved, displacement, arrived, faces,
            )
        else:
            force, reaction = call(
                owner_next_kernel, [force_shape, (block, f32)],
                halved, displacement, arrived, first, nodes,
            )
        returned = to_blocks(exchange(from_blocks(force)))
        (contact,) = call(
            slave_kernel, [(block, f32)],
            [(3, pairs, face_count)] + halved, returned, to_slot, slaves, reaction,
        )
        velocity = velocity + time_step * (internal + contact) / nodal_mass[None]
        displacement = displacement + time_step * velocity
    return (displacement, velocity)


def solution(mesh):
    in_specs = (
        P(None, "len", "wid", "lay"),
        P(None, "len", "wid", "lay"),
        P("len", "wid", "lay"),
        P("len", "wid", "lay"),
        P("len", "wid", "lay"),
        P("len", "wid", "lay", None, None),
        P("len", "wid", "lay", None, None),
        P("len", "wid", "lay", None, None),
        P("len", "wid", "lay", None, None),
        P("len", "wid", "lay", None),
        P("len", "wid", "lay", None, None),
    )
    out_specs = (P(None, "len", "wid", "lay"), P(None, "len", "wid", "lay"))
    return jax.shard_map(
        per_device, mesh=mesh, in_specs=in_specs, out_specs=out_specs, check_vma=False
    )
```

```python
import functools

import jax
import jax.numpy as jnp
from jax import lax
from jax.experimental import pallas as pl
from jax.experimental.pallas import tpu as pltpu
from jax.sharding import PartitionSpec as P

STEPS = 2


penalty = 4.0
hourglass = 0.3
time_step = 0.25
f32 = jnp.float32
bf16 = jnp.bfloat16
CHUNK = 8
MESH = pl.DeviceIdType.MESH


def halves(x):
    high = x.astype(bf16)
    return high, (x - high.astype(f32)).astype(bf16)


def hots(idx, lanes, tall):
    n = idx.shape[1]
    lane = jnp.where(idx < 0, 0, idx % lanes)
    row = jnp.where(idx < 0, -1, idx // lanes)
    lane_iota = lax.broadcasted_iota(jnp.int32, (lanes, n), 0)
    row_iota = lax.broadcasted_iota(jnp.int32, (tall, n), 0)
    lane_hot = jnp.concatenate(
        [jnp.where(lane_iota == lane[j : j + 1, :], 1.0, 0.0).astype(bf16) for j in range(CHUNK)],
        axis=1,
    )
    return lane_hot, [row_iota == row[j : j + 1, :] for j in range(CHUNK)]


def pick(table, lane_hot, match, comps):
    tall, n = match[0].shape
    wide = jnp.dot(
        table, jnp.concatenate([lane_hot, lane_hot], axis=0), preferred_element_type=f32
    )
    out = []
    for c in range(comps):
        rows = []
        for j in range(CHUNK):
            block = wide[c * tall : (c + 1) * tall, j * n : (j + 1) * n]
            rows.append(jnp.sum(jnp.where(match[j], block, 0.0), axis=0, keepdims=True))
        out.append(jnp.concatenate(rows, axis=0))
    return out


def spread(values, lane_hot, match):
    blocks = []
    for v in values:
        for half in halves(v):
            half = half.astype(f32)
            blocks.append(
                jnp.concatenate(
                    [
                        jnp.where(match[j], half[j : j + 1, :], 0.0).astype(bf16)
                        for j in range(CHUNK)
                    ],
                    axis=1,
                )
            )
    return lax.dot_general(
        jnp.concatenate(blocks, axis=0),
        lane_hot,
        (((1,), (1,)), ((), ())),
        preferred_element_type=f32,
    )


def joined(halved, comps, tall):
    return [
        halved[2 * c * tall : (2 * c + 1) * tall] + halved[(2 * c + 1) * tall : (2 * c + 2) * tall]
        for c in range(comps)
    ]


def as_table(blocks):
    both = [halves(b) for b in blocks]
    return jnp.concatenate(
        [
            jnp.concatenate([b[0] for b in both], axis=0),
            jnp.concatenate([b[1] for b in both], axis=0),
        ],
        axis=1,
    )


def exact_dot(a, b):
    return jnp.dot(a, b, precision=lax.Precision.HIGHEST, preferred_element_type=f32)


def flat_block(u, c):
    return jnp.concatenate([u[c, i] for i in range(u.shape[1])], axis=0)


def slot_matrix(col, row, capacity, slots):
    pairs = row.shape[1]
    earlier = lax.broadcasted_iota(jnp.int32, (pairs, pairs), 0) < lax.broadcasted_iota(
        jnp.int32, (pairs, pairs), 1
    )
    rank = jnp.sum(jnp.where((col == row) & earlier, 1.0, 0.0), axis=0, keepdims=True)
    slot = row * capacity + rank.astype(jnp.int32)
    return jnp.where(
        lax.broadcasted_iota(jnp.int32, (slots, pairs), 0) == slot, 1.0, 0.0
    ).astype(f32)


def frames(u):
    span_x, span_y, lanes = u.shape[1:]
    iota_x = lax.broadcasted_iota(jnp.int32, (span_x, span_y, lanes), 0)
    iota_y = lax.broadcasted_iota(jnp.int32, (span_x, span_y, lanes), 1)
    valid = (iota_x < span_x - 1) & (iota_y < span_y - 1)

    def shift_x(v):
        return jnp.concatenate([v[1:], v[:1]], axis=0)

    def shift_y(v):
        return jnp.stack([pltpu.roll(v[i], span_y - 1, 0) for i in range(span_x)])

    one = [u[c] for c in range(3)]
    two = [shift_x(v) for v in one]
    four = [shift_y(v) for v in one]
    three = [shift_x(v) for v in four]
    centroid = [(one[c] + two[c] + three[c] + four[c]) * 0.25 for c in range(3)]
    a = [three[0] - one[0] + 1.0, three[1] - one[1] + 1.0, three[2] - one[2]]
    b = [four[0] - two[0] - 1.0, four[1] - two[1] + 1.0, four[2] - two[2]]
    normal = [
        a[1] * b[2] - a[2] * b[1],
        a[2] * b[0] - a[0] * b[2],
        a[0] * b[1] - a[1] * b[0],
    ]
    square = normal[0] * normal[0] + normal[1] * normal[1] + normal[2] * normal[2]
    usable = valid & (square > 0.0)
    scale = jnp.where(usable, 1.0 / jnp.sqrt(jnp.where(usable, square, 1.0)), 0.0)
    return centroid, [v * scale for v in normal]


def axis_low(shape, dim, span, start, total):
    iota = lax.broadcasted_iota(jnp.int32, shape, dim)
    size = shape[dim]
    low = jnp.where(iota == size - 1, -1, iota)
    inside = (iota < span) | (iota == size - 1)
    return inside & (low + start >= 0) & (low + start <= total - 2)


def next_z(v):
    return pltpu.roll(v, v.shape[1] - 1, 1)


def next_y(v):
    return pltpu.roll(v, v.shape[0] - 1, 0)


def plane_modes(plane):
    ahead = next_z(plane)
    total, diff = ahead + plane, ahead - plane
    total_y, diff_y = next_y(total), next_y(diff)
    return total_y + total, total_y - total, diff_y + diff, diff_y - diff


def fused_kernel(
    sizes,
    u_ref, v_ref, lame_ref, shear_ref, mass_ref, slaves_ref, gap_ref, chosen_ref, col_ref, row_ref,
    patch_ref, faces_ref,
    uo_ref, vo_ref,
    ring, z_in, y_out, y_in, elem, slot_ref, rows_ref, nodes_ref, halved_ref, inner_ref,
    out_1, out_2, in_1, in_2, force_1, force_2, back_1, back_2,
    go_send, go_recv, back_send, back_recv, halo_send, halo_recv,
):
    n_len, n_wid, n_lay = sizes
    groups = n_len * n_wid
    span_x, span_y, span_z = u_ref.shape[1:]
    tall = span_x * span_y
    capacity, n = out_1.shape[2:]
    slots = groups * capacity
    per = CHUNK // capacity
    pairs = slaves_ref.shape[0]
    patches = faces_ref.shape[0]
    ring_y, ring_z = ring.shape[3:]
    at_len, at_wid, at_lay = lax.axis_index("len"), lax.axis_index("wid"), lax.axis_index("lay")
    me = at_len * n_wid + at_wid

    def peer_id(g):
        return (g // n_wid, g % n_wid, at_lay)

    zero_plane = jnp.zeros((ring_y, ring_z), f32)
    for s in range(STEPS):
        for c in range(5 if s == 0 else 3):
            for i in (span_x, span_x + 1):
                ring[s, c, i] = zero_plane

    barrier = pltpu.get_barrier_semaphore()

    def greet(o, _):
        pl.semaphore_signal(
            barrier, inc=1, device_id=peer_id((me + o) % groups), device_id_type=MESH
        )
        return 0

    lax.fori_loop(1, groups, greet, 0)
    lay_peers = [(at_lay + step) % n_lay for step in sorted({1 % n_lay, (n_lay - 1) % n_lay} - {0})]
    for other in lay_peers:
        pl.semaphore_signal(barrier, inc=1, device_id=(at_len, at_wid, other), device_id_type=MESH)
    pl.semaphore_wait(barrier, groups - 1 + len(lay_peers))

    def halo_copy(s, phase, side):
        comps = pl.ds(0, 5 if s == 0 else 3)
        step = 1 if side == 0 else -1
        place = [at_len, at_wid, at_lay]
        axis = 2 - phase
        count = (n_len, n_wid, n_lay)[axis]
        place[axis] = place[axis] + step
        has = (place[axis] >= 0) & (place[axis] < count)
        if phase == 0:
            src = ring.at[s, comps, pl.ds(0, span_x), pl.ds(0, span_y), pl.ds(0, span_z)]
            dst = z_in.at[s, side, comps]
        elif phase == 1:
            src = y_out.at[s, side, comps]
            dst = y_in.at[s, side, comps]
        else:
            src = ring.at[s, comps, span_x - 1 if side == 0 else 0]
            dst = ring.at[s, comps, span_x + 1 if side == 0 else span_x]
        came = [at_len, at_wid, at_lay][axis] - step
        comes = (came >= 0) & (came < count)
        copy = pltpu.make_async_remote_copy(
            src_ref=src,
            dst_ref=dst,
            send_sem=halo_send.at[s, phase, side],
            recv_sem=halo_recv.at[s, phase, side],
            device_id=tuple(place),
            device_id_type=MESH,
        )
        return copy, has, comes

    def halo_start(s, phase):
        for side in range(2):
            copy, has, _ = halo_copy(s, phase, side)

            @pl.when(has)
            def _():
                copy.start()

    def halo_wait(s, phase):
        for side in range(2):
            copy, _, comes = halo_copy(s, phase, side)

            @pl.when(comes)
            def _():
                copy.wait_recv()

    def halo_sent(s):
        for phase in range(3):
            for side in range(2):
                copy, has, _ = halo_copy(s, phase, side)

                @pl.when(has)
                def _():
                    copy.wait_send()

    def go_copy(s, g, slot):
        return pltpu.make_async_remote_copy(
            src_ref=(out_1, out_2)[s].at[g],
            dst_ref=(in_1, in_2)[s].at[slot],
            send_sem=go_send.at[s, g],
            recv_sem=go_recv.at[s, slot],
            device_id=peer_id(g),
            device_id_type=MESH,
        )

    def back_copy(s, g, slot):
        return pltpu.make_async_remote_copy(
            src_ref=(force_1, force_2)[s].at[g],
            dst_ref=(back_1, back_2)[s].at[slot],
            send_sem=back_send.at[s, g],
            recv_sem=back_recv.at[s, slot],
            device_id=peer_id(g),
            device_id_type=MESH,
        )

    def to_groups(rows):
        return rows.reshape(groups, capacity, n)

    def held(ref, b, c):
        return jnp.concatenate([ref[b * per + k, c] for k in range(per)], axis=0)

    faces = faces_ref[...]
    face_table = jnp.concatenate(
        [(faces // n).astype(f32).astype(bf16), (faces % n).astype(f32).astype(bf16)], axis=0
    )
    face_table = jnp.concatenate([face_table, jnp.zeros_like(face_table)], axis=1)
    lanes_z = lax.broadcasted_iota(jnp.int32, (span_y, span_z), 1)
    rows_y = lax.broadcasted_iota(jnp.int32, (ring_y - span_y, ring_z), 0)

    for s in range(STEPS):
        comps = 5 if s == 0 else 3
        now_u, now_v = (u_ref, v_ref) if s == 0 else (uo_ref, vo_ref)
        out, into, force_ref, back = (
            (out_1, in_1, force_1, back_1) if s == 0 else (out_2, in_2, force_2, back_2)
        )
        for c in range(comps):
            for i in range(span_x):
                ring[s, c, i, 0:span_y, 0:span_z] = (
                    now_u[c, i] if c < 3 else (lame_ref, shear_ref)[c - 3][i]
                )
        halo_start(s, 0)

        u = now_u[...]
        table = as_table([flat_block(u, c) for c in range(3)])

        def gather_rows(t, _):
            at = pl.ds(pl.multiple_of(t * CHUNK, CHUNK), CHUNK)
            got = pick(table, *hots(slaves_ref[at, :], span_z, tall), 3)
            for c in range(3):
                rows_ref[c, at, :] = got[c]
            return 0

        lax.fori_loop(0, pairs // CHUNK, gather_rows, 0)
        if s == 0:
            slot_ref[...] = slot_matrix(col_ref[...], row_ref[...], capacity, slots)
            face_id = (patch_ref[...] * n + chosen_ref[...] + 1).astype(f32)
            out[:, 3] = to_groups(exact_dot(slot_ref[...], gap_ref[...]))
            out[:, 4] = to_groups(exact_dot(slot_ref[...], face_id) - 1.0)
        for c in range(3):
            out[:, c] = to_groups(exact_dot(slot_ref[...], rows_ref[c]))
        into[me] = out[me]

        def send_go(o, _):
            go_copy(s, (me + o) % groups, me).start()
            return 0

        lax.fori_loop(1, groups, send_go, 0)

        halo_wait(s, 0)
        for c in range(comps):
            for i in range(span_x):
                tile = jnp.where((lanes_z == 0) & (at_lay + 1 < n_lay), z_in[s, 1, c, i], 0.0)
                tile = jnp.where((lanes_z == span_z - 1) & (at_lay > 0), z_in[s, 0, c, i], tile)
                ring[s, c, i, 0:span_y, span_z:ring_z] = tile
        for c in range(comps):
            for i in range(span_x):
                y_out[s, 0, c, i : i + 1, :] = ring[s, c, i, span_y - 1 : span_y, :]
                y_out[s, 1, c, i : i + 1, :] = ring[s, c, i, 0:1, :]
        halo_start(s, 1)

        centroid, normal = frames(u)
        frame_table = as_table(
            [jnp.concatenate([v[i] for i in range(span_x)], axis=0) for v in centroid + normal]
        )
        halved_ref[...] = jnp.zeros_like(halved_ref)

        halo_wait(s, 1)
        for c in range(comps):
            for i in range(span_x):
                tile = jnp.where(
                    (rows_y == 0) & (at_wid + 1 < n_wid), y_in[s, 1, c, i : i + 1, :], 0.0
                )
                tile = jnp.where(
                    (rows_y == ring_y - span_y - 1) & (at_wid > 0), y_in[s, 0, c, i : i + 1, :], tile
                )
                ring[s, c, i, span_y:ring_y, :] = tile
        halo_start(s, 2)

        def own(t, _):
            b = (me // per - t + groups // per) % (groups // per)
            for k in range(per):
                g = b * per + k

                @pl.when(g != me)
                def _():
                    go_copy(s, g, g).wait_recv()

            if s == 0:
                face_id = held(in_1, b, 4).astype(jnp.int32)
                high, low = pick(face_table, *hots(face_id, n, patches), 2)
                node = high.astype(jnp.int32) * span_z + low.astype(jnp.int32)
                nodes_ref[b] = jnp.where(face_id < 0, -1, node)
            lane_hot, match = hots(nodes_ref[b], span_z, tall)
            got = pick(frame_table, lane_hot, match, 6)
            gap = held(in_1, b, 3)
            for c in range(3):
                gap = gap + (held(into, b, c) - got[c]) * got[3 + c]
            push = -penalty * jnp.minimum(gap, 0.0)
            force = [push * got[3 + c] for c in range(3)]
            for c in range(3):
                for k in range(per):
                    force_ref[b * per + k, c] = force[c][k * capacity : (k + 1) * capacity]
            for k in range(per):
                g = b * per + k

                @pl.when(g != me)
                def _():
                    back_copy(s, g, me).start()

            halved_ref[...] += spread(force, lane_hot, match)
            return 0

        lax.fori_loop(0, groups // per, own, 0)
        back[me] = force_ref[me]

        total = joined(halved_ref[...], 3, tall)
        zero = jnp.zeros((span_y, span_z), f32)
        for c in range(3):
            quarter = [-0.25 * total[c][i * span_y : (i + 1) * span_y] for i in range(span_x)]
            for i in range(span_x):
                both = (quarter[i] if i < span_x - 1 else zero) + (quarter[i - 1] if i else zero)
                inner_ref[c, i] = both + pltpu.roll(both, 1, 0)

        halo_wait(s, 2)
        planes = [span_x + 1] + list(range(span_x + 1))
        if s == 0:
            shape = (ring_y, ring_z)
            valid = axis_low(shape, 0, span_y, at_wid * span_y, n_wid * span_y) & axis_low(
                shape, 1, span_z, at_lay * span_z, n_lay * span_z
            )
            for m in range(2):
                sums = [plane_modes(ring[0, 3 + m, i])[0] for i in planes]
                for e in range(span_x + 1):
                    low = at_len * span_x + e - 1
                    there = valid & (low >= 0) & (low <= n_len * span_x - 2)
                    elem[m, e] = jnp.where(there, (sums[e] + sums[e + 1]) * 0.125, 0.0)
        below = [plane_modes(ring[s, c, planes[0]]) for c in range(3)]
        carried = None
        for e in range(span_x + 1):
            above = [plane_modes(ring[s, c, planes[e + 1]]) for c in range(3)]
            lame, shear = elem[0, e], elem[1, e]
            grad = [
                [
                    0.25 * (above[c][0] - below[c][0]),
                    0.25 * (above[c][1] + below[c][1]),
                    0.25 * (above[c][2] + below[c][2]),
                ]
                for c in range(3)
            ]
            pressure = lame * (grad[0][0] + grad[1][1] + grad[2][2])
            sheared = -0.25 * shear
            damped = (-0.125 * hourglass) * shear
            lower, upper = [], []
            for c in range(3):
                lin = [sheared * (grad[c][j] + grad[j][c]) for j in range(3)]
                lin[c] = lin[c] - 0.25 * pressure
                h_xy = damped * (above[c][1] - below[c][1])
                h_xz = damped * (above[c][2] - below[c][2])
                h_yz = damped * (above[c][3] + below[c][3])
                h_xyz = damped * (above[c][3] - below[c][3])
                lower.append([-lin[0], lin[1] - h_xy, lin[2] - h_xz, h_yz - h_xyz])
                upper.append([lin[0], lin[1] + h_xy, lin[2] + h_xz, h_yz + h_xyz])
            if e > 0:
                for c in range(3):
                    none, y, z, yz = [a + b for a, b in zip(carried[c], lower[c])]
                    even = pltpu.roll(none + z, 1, 1) + (none - z)
                    odd = pltpu.roll(y + yz, 1, 1) + (y - yz)
                    node = pltpu.roll(even + odd, 1, 0) + (even - odd)
                    inner_ref[c, e - 1] += node[0:span_y, 0:span_z]
            carried, below = upper, above

        def wait_back(o, _):
            g = (me + o) % groups
            back_copy(s, g, g).wait_recv()
            return 0

        lax.fori_loop(1, groups, wait_back, 0)
        for c in range(3):
            rows_ref[c] = lax.dot_general(
                slot_ref[...],
                back[:, c].reshape(slots, n),
                (((0,), (0,)), ((), ())),
                precision=lax.Precision.HIGHEST,
                preferred_element_type=f32,
            )
        halved_ref[...] = jnp.zeros_like(halved_ref)

        def scatter_rows(t, _):
            at = pl.ds(pl.multiple_of(t * CHUNK, CHUNK), CHUNK)
            halved_ref[...] += spread(
                [rows_ref[c, at, :] for c in range(3)], *hots(slaves_ref[at, :], span_z, tall)
            )
            return 0

        lax.fori_loop(0, pairs // CHUNK, scatter_rows, 0)
        total = joined(halved_ref[...], 3, tall)
        for i in range(span_x):
            rate = time_step / mass_ref[i]
            for c in range(3):
                force = inner_ref[c, i] + total[c][i * span_y : (i + 1) * span_y]
                speed = now_v[c, i] + rate * force
                vo_ref[c, i] = speed
                uo_ref[c, i] = now_u[c, i] + time_step * speed

    for s in range(STEPS):
        halo_sent(s)

        def sent(o, _):
            g = (me + o) % groups
            go_copy(s, g, me).wait_send()
            back_copy(s, g, me).wait_send()
            return 0

        lax.fori_loop(1, groups, sent, 0)


def per_device(
    displacement,
    velocity,
    lame_first,
    shear_modulus,
    nodal_mass,
    slave_nodes,
    initial_gap,
    candidate,
    pair_owner,
    pair_patch,
    master_faces,
):
    span_x, span_y, span_z = displacement.shape[1:]
    sizes = tuple(lax.axis_size(a) for a in ("len", "wid", "lay"))
    groups = sizes[0] * sizes[1]
    pairs, n = slave_nodes.shape[3:]
    patches = master_faces.shape[3]
    capacity = max(2, 2 * pairs // groups)
    slots = groups * capacity
    tall = span_x * span_y
    ring_y, ring_z = span_y + 8, span_z + 128
    args = (
        displacement,
        velocity,
        lame_first,
        shear_modulus,
        nodal_mass,
        slave_nodes.reshape(pairs, n),
        initial_gap.reshape(pairs, n),
        candidate.reshape(pairs, n),
        pair_owner.reshape(pairs, 1),
        pair_owner.reshape(1, pairs),
        pair_patch.reshape(pairs, 1),
        master_faces.reshape(patches, n),
    )
    block = (3, span_x, span_y, span_z)
    vm = lambda *shape: pltpu.VMEM(shape, f32)
    wide, slim = (groups, 5, capacity, n), (groups, 3, capacity, n)
    dma = lambda *shape: pltpu.SemaphoreType.DMA(shape)
    return pl.pallas_call(
        functools.partial(fused_kernel, sizes),
        out_shape=[jax.ShapeDtypeStruct(block, f32)] * 2,
        in_specs=[pl.BlockSpec(memory_space=pltpu.VMEM)] * len(args),
        out_specs=[pl.BlockSpec(memory_space=pltpu.VMEM)] * 2,
        scratch_shapes=[
            vm(STEPS, 5, span_x + 2, ring_y, ring_z),
            vm(STEPS, 2, 5, span_x, span_y, span_z),
            vm(STEPS, 2, 5, span_x, ring_z),
            vm(STEPS, 2, 5, span_x, ring_z),
            vm(2, span_x + 1, ring_y, ring_z),
            vm(slots, pairs),
            vm(3, pairs, n),
            pltpu.VMEM((slots // CHUNK, CHUNK, n), jnp.int32),
            vm(6 * tall, span_z),
            vm(*block),
            vm(*wide), vm(*slim), vm(*wide), vm(*slim),
            vm(*slim), vm(*slim), vm(*slim), vm(*slim),
            dma(STEPS, groups), dma(STEPS, groups), dma(STEPS, groups), dma(STEPS, groups),
            dma(STEPS, 3, 2), dma(STEPS, 3, 2),
        ],
        compiler_params=pltpu.CompilerParams(
            collective_id=0, has_side_effects=True, vmem_limit_bytes=48 * 1024 * 1024
        ),
    )(*args)


def solution(mesh):
    in_specs = (
        P(None, "len", "wid", "lay"),
        P(None, "len", "wid", "lay"),
        P("len", "wid", "lay"),
        P("len", "wid", "lay"),
        P("len", "wid", "lay"),
        P("len", "wid", "lay", None, None),
        P("len", "wid", "lay", None, None),
        P("len", "wid", "lay", None, None),
        P("len", "wid", "lay", None, None),
        P("len", "wid", "lay", None),
        P("len", "wid", "lay", None, None),
    )
    out_specs = (P(None, "len", "wid", "lay"), P(None, "len", "wid", "lay"))
    return jax.shard_map(
        per_device, mesh=mesh, in_specs=in_specs, out_specs=out_specs, check_vma=False
    )
```

```python
import functools

import jax
import jax.numpy as jnp
from jax import lax
from jax.experimental import pallas as pl
from jax.experimental.pallas import tpu as pltpu
from jax.sharding import PartitionSpec as P

STEPS = 2


penalty = 4.0
hourglass = 0.3
time_step = 0.25
f32 = jnp.float32
bf16 = jnp.bfloat16
CHUNK = 8
MESH = pl.DeviceIdType.MESH


def halves(x):
    high = x.astype(bf16)
    return high, (x - high.astype(f32)).astype(bf16)


def hots(idx, lanes, tall):
    n = idx.shape[1]
    lane = jnp.where(idx < 0, 0, idx % lanes)
    row = jnp.where(idx < 0, -1, idx // lanes)
    lane_iota = lax.broadcasted_iota(jnp.int32, (lanes, n), 0)
    row_iota = lax.broadcasted_iota(jnp.int32, (tall, n), 0)
    lane_hot = jnp.concatenate(
        [jnp.where(lane_iota == lane[j : j + 1, :], 1.0, 0.0).astype(bf16) for j in range(CHUNK)],
        axis=1,
    )
    return lane_hot, [row_iota == row[j : j + 1, :] for j in range(CHUNK)]


def pick(table, lane_hot, match, comps):
    tall, n = match[0].shape
    wide = jnp.dot(
        table, jnp.concatenate([lane_hot, lane_hot], axis=0), preferred_element_type=f32
    )
    out = []
    for c in range(comps):
        rows = []
        for j in range(CHUNK):
            block = wide[c * tall : (c + 1) * tall, j * n : (j + 1) * n]
            rows.append(jnp.sum(jnp.where(match[j], block, 0.0), axis=0, keepdims=True))
        out.append(jnp.concatenate(rows, axis=0))
    return out


def spread(values, lane_hot, match):
    blocks = []
    for v in values:
        for half in halves(v):
            half = half.astype(f32)
            blocks.append(
                jnp.concatenate(
                    [
                        jnp.where(match[j], half[j : j + 1, :], 0.0).astype(bf16)
                        for j in range(CHUNK)
                    ],
                    axis=1,
                )
            )
    return lax.dot_general(
        jnp.concatenate(blocks, axis=0),
        lane_hot,
        (((1,), (1,)), ((), ())),
        preferred_element_type=f32,
    )


def joined(halved, comps, tall):
    return [
        halved[2 * c * tall : (2 * c + 1) * tall] + halved[(2 * c + 1) * tall : (2 * c + 2) * tall]
        for c in range(comps)
    ]


def as_table(blocks):
    both = [halves(b) for b in blocks]
    return jnp.concatenate(
        [
            jnp.concatenate([b[0] for b in both], axis=0),
            jnp.concatenate([b[1] for b in both], axis=0),
        ],
        axis=1,
    )


def exact_dot(a, b):
    return jnp.dot(a, b, precision=lax.Precision.HIGHEST, preferred_element_type=f32)


def flat_block(u, c):
    return jnp.concatenate([u[c, i] for i in range(u.shape[1])], axis=0)


def slot_matrix(col, row, capacity, slots):
    pairs = row.shape[1]
    earlier = lax.broadcasted_iota(jnp.int32, (pairs, pairs), 0) < lax.broadcasted_iota(
        jnp.int32, (pairs, pairs), 1
    )
    rank = jnp.sum(jnp.where((col == row) & earlier, 1.0, 0.0), axis=0, keepdims=True)
    slot = row * capacity + rank.astype(jnp.int32)
    return jnp.where(
        lax.broadcasted_iota(jnp.int32, (slots, pairs), 0) == slot, 1.0, 0.0
    ).astype(f32)


def frames(u):
    span_x, span_y, lanes = u.shape[1:]
    iota_x = lax.broadcasted_iota(jnp.int32, (span_x, span_y, lanes), 0)
    iota_y = lax.broadcasted_iota(jnp.int32, (span_x, span_y, lanes), 1)
    valid = (iota_x < span_x - 1) & (iota_y < span_y - 1)

    def shift_x(v):
        return jnp.concatenate([v[1:], v[:1]], axis=0)

    def shift_y(v):
        return jnp.stack([pltpu.roll(v[i], span_y - 1, 0) for i in range(span_x)])

    one = [u[c] for c in range(3)]
    two = [shift_x(v) for v in one]
    four = [shift_y(v) for v in one]
    three = [shift_x(v) for v in four]
    centroid = [(one[c] + two[c] + three[c] + four[c]) * 0.25 for c in range(3)]
    a = [three[0] - one[0] + 1.0, three[1] - one[1] + 1.0, three[2] - one[2]]
    b = [four[0] - two[0] - 1.0, four[1] - two[1] + 1.0, four[2] - two[2]]
    normal = [
        a[1] * b[2] - a[2] * b[1],
        a[2] * b[0] - a[0] * b[2],
        a[0] * b[1] - a[1] * b[0],
    ]
    square = normal[0] * normal[0] + normal[1] * normal[1] + normal[2] * normal[2]
    usable = valid & (square > 0.0)
    scale = jnp.where(usable, 1.0 / jnp.sqrt(jnp.where(usable, square, 1.0)), 0.0)
    return centroid, [v * scale for v in normal]


def axis_low(shape, dim, span, start, total):
    iota = lax.broadcasted_iota(jnp.int32, shape, dim)
    size = shape[dim]
    low = jnp.where(iota == size - 1, -1, iota)
    inside = (iota < span) | (iota == size - 1)
    return inside & (low + start >= 0) & (low + start <= total - 2)


def next_z(v):
    return pltpu.roll(v, v.shape[1] - 1, 1)


def next_y(v):
    return pltpu.roll(v, v.shape[0] - 1, 0)


def plane_modes(plane):
    ahead = next_z(plane)
    total, diff = ahead + plane, ahead - plane
    total_y, diff_y = next_y(total), next_y(diff)
    return total_y + total, total_y - total, diff_y + diff, diff_y - diff


def fused_kernel(
    sizes,
    u_hbm, v_hbm, lame_hbm, shear_hbm, mass_hbm, slaves_hbm, gap_hbm, chosen_hbm, row_hbm,
    patch_hbm, faces_hbm,
    uo_ref, vo_ref,
    u_ref, v_ref, lame_ref, shear_ref, mass_ref, slaves_ref, gap_ref, chosen_ref, row_ref,
    patch_ref, faces_ref, load_sem,
    ring, z_in, y_out, y_in, elem, slot_ref, rows_ref, nodes_ref, halved_ref, inner_ref,
    fix_out, fix_in, out_1, out_2, in_1, in_2, force_1, force_2, back_1, back_2,
    fix_send, fix_recv, go_send, go_recv, back_send, back_recv, halo_send, halo_recv,
):
    n_len, n_wid, n_lay = sizes
    groups = n_len * n_wid
    span_x, span_y, span_z = u_ref.shape[1:]
    tall = span_x * span_y
    capacity, n = out_1.shape[2:]
    slots = groups * capacity
    per = CHUNK // capacity
    pairs = slaves_ref.shape[0]
    patches = faces_ref.shape[0]
    ring_y, ring_z = ring.shape[3:]
    blocks = groups // per
    side_by = 2 if blocks % 2 == 0 and pairs // CHUNK % 2 == 0 else 1
    at_len, at_wid, at_lay = lax.axis_index("len"), lax.axis_index("wid"), lax.axis_index("lay")
    me = at_len * n_wid + at_wid

    def peer_id(g):
        return (g // n_wid, g % n_wid, at_lay)

    loads = [
        pltpu.make_async_copy(src, dst, load_sem.at[i])
        for i, (src, dst) in enumerate(
            (
                (row_hbm, row_ref), (patch_hbm, patch_ref), (gap_hbm, gap_ref),
                (chosen_hbm, chosen_ref), (u_hbm, u_ref), (slaves_hbm, slaves_ref),
                (lame_hbm, lame_ref), (shear_hbm, shear_ref), (faces_hbm, faces_ref),
                (v_hbm, v_ref), (mass_hbm, mass_ref),
            )
        )
    ]
    for load in loads:
        load.start()

    zero_plane = jnp.zeros((ring_y, ring_z), f32)
    for s in range(STEPS):
        for c in range(5 if s == 0 else 3):
            for i in (span_x, span_x + 1):
                ring[s, c, i] = zero_plane

    barrier = pltpu.get_barrier_semaphore()

    def greet(o, _):
        pl.semaphore_signal(
            barrier, inc=1, device_id=peer_id((me + o) % groups), device_id_type=MESH
        )
        return 0

    lax.fori_loop(1, groups, greet, 0)
    lay_peers = [(at_lay + step) % n_lay for step in sorted({1 % n_lay, (n_lay - 1) % n_lay} - {0})]
    for other in lay_peers:
        pl.semaphore_signal(barrier, inc=1, device_id=(at_len, at_wid, other), device_id_type=MESH)
    pl.semaphore_wait(barrier, groups - 1 + len(lay_peers))
    for load in loads:
        load.wait()

    def halo_copy(s, phase, side):
        comps = pl.ds(0, 5 if s == 0 else 3)
        step = 1 if side == 0 else -1
        place = [at_len, at_wid, at_lay]
        axis = 2 - phase
        count = (n_len, n_wid, n_lay)[axis]
        place[axis] = place[axis] + step
        has = (place[axis] >= 0) & (place[axis] < count)
        if phase == 0:
            src = ring.at[s, comps, pl.ds(0, span_x), pl.ds(0, span_y), pl.ds(0, span_z)]
            dst = z_in.at[s, side, comps]
        elif phase == 1:
            src = y_out.at[s, side, comps]
            dst = y_in.at[s, side, comps]
        else:
            src = ring.at[s, comps, span_x - 1 if side == 0 else 0]
            dst = ring.at[s, comps, span_x + 1 if side == 0 else span_x]
        came = [at_len, at_wid, at_lay][axis] - step
        comes = (came >= 0) & (came < count)
        copy = pltpu.make_async_remote_copy(
            src_ref=src,
            dst_ref=dst,
            send_sem=halo_send.at[s, phase, side],
            recv_sem=halo_recv.at[s, phase, side],
            device_id=tuple(place),
            device_id_type=MESH,
        )
        return copy, has, comes

    def halo_start(s, phase):
        for side in range(2):
            copy, has, _ = halo_copy(s, phase, side)

            @pl.when(has)
            def _():
                copy.start()

    def halo_wait(s, phase):
        for side in range(2):
            copy, _, comes = halo_copy(s, phase, side)

            @pl.when(comes)
            def _():
                copy.wait_recv()

    def halo_sent(s):
        for phase in range(3):
            for side in range(2):
                copy, has, _ = halo_copy(s, phase, side)

                @pl.when(has)
                def _():
                    copy.wait_send()

    def fix_copy(g, slot):
        return pltpu.make_async_remote_copy(
            src_ref=fix_out.at[g],
            dst_ref=fix_in.at[slot],
            send_sem=fix_send.at[g],
            recv_sem=fix_recv.at[slot],
            device_id=peer_id(g),
            device_id_type=MESH,
        )

    def go_copy(s, g, slot):
        return pltpu.make_async_remote_copy(
            src_ref=(out_1, out_2)[s].at[g],
            dst_ref=(in_1, in_2)[s].at[slot],
            send_sem=go_send.at[s, g],
            recv_sem=go_recv.at[s, slot],
            device_id=peer_id(g),
            device_id_type=MESH,
        )

    def back_copy(s, g, slot):
        return pltpu.make_async_remote_copy(
            src_ref=(force_1, force_2)[s].at[g],
            dst_ref=(back_1, back_2)[s].at[slot],
            send_sem=back_send.at[s, g],
            recv_sem=back_recv.at[s, slot],
            device_id=peer_id(g),
            device_id_type=MESH,
        )

    def to_groups(rows):
        return rows.reshape(groups, capacity, n)

    def held(ref, b, c):
        return jnp.concatenate([ref[b * per + k, c] for k in range(per)], axis=0)

    faces = faces_ref[...]
    face_table = jnp.concatenate(
        [(faces // n).astype(f32).astype(bf16), (faces % n).astype(f32).astype(bf16)], axis=0
    )
    face_table = jnp.concatenate([face_table, jnp.zeros_like(face_table)], axis=1)
    lanes_z = lax.broadcasted_iota(jnp.int32, (span_y, span_z), 1)
    rows_y = lax.broadcasted_iota(jnp.int32, (ring_y - span_y, ring_z), 0)

    diagonal = lax.broadcasted_iota(jnp.int32, (pairs, pairs), 0) == lax.broadcasted_iota(
        jnp.int32, (pairs, pairs), 1
    )

    def column(row):
        return jnp.sum(jnp.where(diagonal, row.astype(f32), 0.0), axis=1, keepdims=True).astype(
            jnp.int32
        )

    row = row_ref[...]
    to_slot = slot_matrix(column(row), row, capacity, slots)
    slot_ref[...] = jnp.concatenate([to_slot, to_slot], axis=1).astype(bf16)
    face_id = (column(patch_ref[...]) * n + chosen_ref[...] + 1).astype(f32)
    fix_out[:, 0] = to_groups(exact_dot(to_slot, gap_ref[...]))
    fix_out[:, 1] = to_groups(exact_dot(to_slot, face_id) - 1.0)
    fix_in[me] = fix_out[me]

    for s in range(STEPS):
        comps = 5 if s == 0 else 3
        now_u, now_v = (u_ref, v_ref) if s == 0 else (uo_ref, vo_ref)
        out, into, force_ref, back = (
            (out_1, in_1, force_1, back_1) if s == 0 else (out_2, in_2, force_2, back_2)
        )
        for c in range(comps):
            for i in range(span_x):
                ring[s, c, i, 0:span_y, 0:span_z] = (
                    now_u[c, i] if c < 3 else (lame_ref, shear_ref)[c - 3][i]
                )
        halo_start(s, 0)
        if s == 0:

            def send_fix(o, _):
                fix_copy((me + o) % groups, me).start()
                return 0

            lax.fori_loop(1, groups, send_fix, 0)

        u = now_u[...]
        table = as_table([flat_block(u, c) for c in range(3)])

        to_slots = slot_ref[...]

        def gather_rows(t, _):
            for q in range(side_by):
                at = pl.ds(pl.multiple_of((t * side_by + q) * CHUNK, CHUNK), CHUNK)
                got = pick(table, *hots(slaves_ref[at, :], span_z, tall), 3)
                for c in range(3):
                    rows_ref[c, at, :] = got[c]
            return 0

        lax.fori_loop(0, pairs // CHUNK // side_by, gather_rows, 0)
        both = [halves(rows_ref[c]) for c in range(3)]
        moved = jnp.dot(
            to_slots,
            jnp.concatenate([jnp.concatenate([b[k] for b in both], axis=1) for k in range(2)], axis=0),
            preferred_element_type=f32,
        )
        for c in range(3):
            out[:, c] = to_groups(moved[:, c * n : (c + 1) * n])
        into[me] = out[me]

        def send_go(o, _):
            go_copy(s, (me + o) % groups, me).start()
            return 0

        lax.fori_loop(1, groups, send_go, 0)

        halo_wait(s, 0)
        for c in range(comps):
            for i in range(span_x):
                tile = jnp.where((lanes_z == 0) & (at_lay + 1 < n_lay), z_in[s, 1, c, i], 0.0)
                tile = jnp.where((lanes_z == span_z - 1) & (at_lay > 0), z_in[s, 0, c, i], tile)
                ring[s, c, i, 0:span_y, span_z:ring_z] = tile
        for c in range(comps):
            for i in range(span_x):
                y_out[s, 0, c, i : i + 1, :] = ring[s, c, i, span_y - 1 : span_y, :]
                y_out[s, 1, c, i : i + 1, :] = ring[s, c, i, 0:1, :]
        halo_start(s, 1)

        centroid, normal = frames(u)
        frame_table = as_table(
            [jnp.concatenate([v[i] for i in range(span_x)], axis=0) for v in centroid + normal]
        )
        halved_ref[...] = jnp.zeros_like(halved_ref)

        halo_wait(s, 1)
        for c in range(comps):
            for i in range(span_x):
                tile = jnp.where(
                    (rows_y == 0) & (at_wid + 1 < n_wid), y_in[s, 1, c, i : i + 1, :], 0.0
                )
                tile = jnp.where(
                    (rows_y == ring_y - span_y - 1) & (at_wid > 0), y_in[s, 0, c, i : i + 1, :], tile
                )
                ring[s, c, i, span_y:ring_y, :] = tile
        halo_start(s, 2)

        planes = [span_x + 1] + list(range(span_x + 1))
        shape = (ring_y, ring_z)

        def material(e):
            valid = axis_low(shape, 0, span_y, at_wid * span_y, n_wid * span_y) & axis_low(
                shape, 1, span_z, at_lay * span_z, n_lay * span_z
            )
            low = at_len * span_x + e - 1
            there = valid & (low >= 0) & (low <= n_len * span_x - 2)
            for m in range(2):
                sums = [plane_modes(ring[0, 3 + m, planes[e + k]])[0] for k in range(2)]
                elem[m, e] = jnp.where(there, (sums[0] + sums[1]) * 0.125, 0.0)

        def settle(i, modes):
            for c in range(3):
                none, y, z, yz = modes[c]
                even = pltpu.roll(none + z, 1, 1) + (none - z)
                odd = pltpu.roll(y + yz, 1, 1) + (y - yz)
                node = pltpu.roll(even + odd, 1, 0) + (even - odd)
                inner_ref[c, i] += node[0:span_y, 0:span_z]

        def internal(elements):
            carried, last = None, None
            for e in elements:
                if s == 0:
                    material(e)
                if e - 1 == last:
                    below = above
                else:
                    if carried is not None and last < span_x:
                        settle(last, carried)
                    carried = None
                    below = [plane_modes(ring[s, c, planes[e]]) for c in range(3)]
                above = [plane_modes(ring[s, c, planes[e + 1]]) for c in range(3)]
                lame, shear = elem[0, e], elem[1, e]
                grad = [
                    [
                        0.25 * (above[c][0] - below[c][0]),
                        0.25 * (above[c][1] + below[c][1]),
                        0.25 * (above[c][2] + below[c][2]),
                    ]
                    for c in range(3)
                ]
                pressure = lame * (grad[0][0] + grad[1][1] + grad[2][2])
                sheared = -0.25 * shear
                damped = (-0.125 * hourglass) * shear
                lower, upper = [], []
                for c in range(3):
                    lin = [sheared * (grad[c][j] + grad[j][c]) for j in range(3)]
                    lin[c] = lin[c] - 0.25 * pressure
                    h_xy = damped * (above[c][1] - below[c][1])
                    h_xz = damped * (above[c][2] - below[c][2])
                    h_yz = damped * (above[c][3] + below[c][3])
                    h_xyz = damped * (above[c][3] - below[c][3])
                    lower.append([-lin[0], lin[1] - h_xy, lin[2] - h_xz, h_yz - h_xyz])
                    upper.append([lin[0], lin[1] + h_xy, lin[2] + h_xz, h_yz + h_xyz])
                if e > 0:
                    if carried is None:
                        settle(e - 1, lower)
                    else:
                        settle(e - 1, [[p + q for p, q in zip(carried[c], lower[c])] for c in range(3)])
                carried, last = upper, e
            if last < span_x:
                settle(last, carried)

        inner_ref[...] = jnp.zeros_like(inner_ref)
        internal(list(range(1, span_x)))

        def landed(t):
            return [(me // per - t * side_by - q + 2 * blocks) % blocks for q in range(side_by)]

        def others(t, act):
            for b in landed(t):
                for k in range(per):
                    g = b * per + k

                    @pl.when(g != me)
                    def _():
                        act(g)

        if s == 0:

            def resolve(t, _):
                others(t, lambda g: fix_copy(g, g).wait_recv())
                for b in landed(t):
                    face_id = held(fix_in, b, 1).astype(jnp.int32)
                    high, low = pick(face_table, *hots(face_id, n, patches), 2)
                    node = high.astype(jnp.int32) * span_z + low.astype(jnp.int32)
                    nodes_ref[b] = jnp.where(face_id < 0, -1, node)
                return 0

            lax.fori_loop(0, blocks // side_by, resolve, 0)

        def own(t, _):
            others(t, lambda g: go_copy(s, g, g).wait_recv())
            added = []
            for b in landed(t):
                lane_hot, match = hots(nodes_ref[b], span_z, tall)
                got = pick(frame_table, lane_hot, match, 6)
                gap = held(fix_in, b, 0)
                for c in range(3):
                    gap = gap + (held(into, b, c) - got[c]) * got[3 + c]
                push = -penalty * jnp.minimum(gap, 0.0)
                force = [push * got[3 + c] for c in range(3)]
                for c in range(3):
                    for k in range(per):
                        force_ref[b * per + k, c] = force[c][k * capacity : (k + 1) * capacity]
                added.append(spread(force, lane_hot, match))
            others(t, lambda g: back_copy(s, g, me).start())
            halved_ref[...] += functools.reduce(jnp.add, added)
            return 0

        lax.fori_loop(0, blocks // side_by, own, 0)
        back[me] = force_ref[me]

        total = joined(halved_ref[...], 3, tall)
        zero = jnp.zeros((span_y, span_z), f32)
        for c in range(3):
            quarter = [-0.25 * total[c][i * span_y : (i + 1) * span_y] for i in range(span_x)]
            for i in range(span_x):
                both = (quarter[i] if i < span_x - 1 else zero) + (quarter[i - 1] if i else zero)
                inner_ref[c, i] += both + pltpu.roll(both, 1, 0)

        halo_wait(s, 2)
        internal([0, span_x])

        def wait_back(o, _):
            g = (me + o) % groups
            back_copy(s, g, g).wait_recv()
            return 0

        lax.fori_loop(1, groups, wait_back, 0)
        both = [halves(back[:, c].reshape(slots, n)) for c in range(3)]
        moved = lax.dot_general(
            to_slots[:, 0:pairs],
            jnp.concatenate([b[k] for k in range(2) for b in both], axis=1),
            (((0,), (0,)), ((), ())),
            preferred_element_type=f32,
        )
        for c in range(3):
            rows_ref[c] = moved[:, c * n : (c + 1) * n] + moved[:, (3 + c) * n : (4 + c) * n]
        halved_ref[...] = jnp.zeros_like(halved_ref)

        def scatter_rows(t, _):
            added = []
            for q in range(side_by):
                at = pl.ds(pl.multiple_of((t * side_by + q) * CHUNK, CHUNK), CHUNK)
                added.append(
                    spread(
                        [rows_ref[c, at, :] for c in range(3)],
                        *hots(slaves_ref[at, :], span_z, tall),
                    )
                )
            halved_ref[...] += functools.reduce(jnp.add, added)
            return 0

        lax.fori_loop(0, pairs // CHUNK // side_by, scatter_rows, 0)
        total = joined(halved_ref[...], 3, tall)
        for i in range(span_x):
            rate = time_step / mass_ref[i]
            for c in range(3):
                force = inner_ref[c, i] + total[c][i * span_y : (i + 1) * span_y]
                speed = now_v[c, i] + rate * force
                vo_ref[c, i] = speed
                uo_ref[c, i] = now_u[c, i] + time_step * speed

    for s in range(STEPS):
        halo_sent(s)

        def sent(o, _):
            g = (me + o) % groups
            if s == 0:
                fix_copy(g, me).wait_send()
            go_copy(s, g, me).wait_send()
            back_copy(s, g, me).wait_send()
            return 0

        lax.fori_loop(1, groups, sent, 0)


def per_device(
    displacement,
    velocity,
    lame_first,
    shear_modulus,
    nodal_mass,
    slave_nodes,
    initial_gap,
    candidate,
    pair_owner,
    pair_patch,
    master_faces,
):
    span_x, span_y, span_z = displacement.shape[1:]
    sizes = tuple(lax.axis_size(a) for a in ("len", "wid", "lay"))
    groups = sizes[0] * sizes[1]
    pairs, n = slave_nodes.shape[3:]
    patches = master_faces.shape[3]
    capacity = max(2, 2 * pairs // groups)
    slots = groups * capacity
    tall = span_x * span_y
    ring_y, ring_z = span_y + 8, span_z + 128
    args = (
        displacement,
        velocity,
        lame_first,
        shear_modulus,
        nodal_mass,
        slave_nodes.reshape(pairs, n),
        initial_gap.reshape(pairs, n),
        candidate.reshape(pairs, n),
        pair_owner.reshape(1, pairs),
        pair_patch.reshape(1, pairs),
        master_faces.reshape(patches, n),
    )
    block = (3, span_x, span_y, span_z)
    vm = lambda *shape: pltpu.VMEM(shape, f32)
    fixed, slim = (groups, 2, capacity, n), (groups, 3, capacity, n)
    dma = lambda *shape: pltpu.SemaphoreType.DMA(shape)
    return pl.pallas_call(
        functools.partial(fused_kernel, sizes),
        out_shape=[jax.ShapeDtypeStruct(block, f32)] * 2,
        in_specs=[pl.BlockSpec(memory_space=pltpu.HBM)] * len(args),
        out_specs=[pl.BlockSpec(memory_space=pltpu.VMEM)] * 2,
        scratch_shapes=[
            *[pltpu.VMEM(a.shape, a.dtype) for a in args],
            dma(len(args)),
            vm(STEPS, 5, span_x + 2, ring_y, ring_z),
            vm(STEPS, 2, 5, span_x, span_y, span_z),
            vm(STEPS, 2, 5, span_x, ring_z),
            vm(STEPS, 2, 5, span_x, ring_z),
            vm(2, span_x + 1, ring_y, ring_z),
            pltpu.VMEM((slots, 2 * pairs), bf16),
            vm(3, pairs, n),
            pltpu.VMEM((slots // CHUNK, CHUNK, n), jnp.int32),
            vm(6 * tall, span_z),
            vm(*block),
            vm(*fixed), vm(*fixed), vm(*slim), vm(*slim), vm(*slim), vm(*slim),
            vm(*slim), vm(*slim), vm(*slim), vm(*slim),
            dma(groups), dma(groups),
            dma(STEPS, groups), dma(STEPS, groups), dma(STEPS, groups), dma(STEPS, groups),
            dma(STEPS, 3, 2), dma(STEPS, 3, 2),
        ],
        compiler_params=pltpu.CompilerParams(
            collective_id=0, has_side_effects=True, vmem_limit_bytes=48 * 1024 * 1024
        ),
    )(*args)


def solution(mesh):
    in_specs = (
        P(None, "len", "wid", "lay"),
        P(None, "len", "wid", "lay"),
        P("len", "wid", "lay"),
        P("len", "wid", "lay"),
        P("len", "wid", "lay"),
        P("len", "wid", "lay", None, None),
        P("len", "wid", "lay", None, None),
        P("len", "wid", "lay", None, None),
        P("len", "wid", "lay", None, None),
        P("len", "wid", "lay", None),
        P("len", "wid", "lay", None, None),
    )
    out_specs = (P(None, "len", "wid", "lay"), P(None, "len", "wid", "lay"))
    return jax.shard_map(
        per_device, mesh=mesh, in_specs=in_specs, out_specs=out_specs, check_vma=False
    )
```

```python
import functools

import jax
import jax.numpy as jnp
from jax import lax
from jax.experimental import pallas as pl
from jax.experimental.pallas import tpu as pltpu
from jax.sharding import PartitionSpec as P

STEPS = 2


penalty = 4.0
hourglass = 0.3
time_step = 0.25
f32 = jnp.float32
bf16 = jnp.bfloat16
CHUNK = 8
MESH = pl.DeviceIdType.MESH


def halves(x):
    high = x.astype(bf16)
    return high, (x - high.astype(f32)).astype(bf16)


def hots(idx, lanes, tall):
    n = idx.shape[1]
    lane = jnp.where(idx < 0, 0, idx % lanes)
    row = jnp.where(idx < 0, -1, idx // lanes)
    lane_iota = lax.broadcasted_iota(jnp.int32, (lanes, n), 0)
    row_iota = lax.broadcasted_iota(jnp.int32, (tall, n), 0)
    lane_hot = jnp.concatenate(
        [jnp.where(lane_iota == lane[j : j + 1, :], 1.0, 0.0).astype(bf16) for j in range(CHUNK)],
        axis=1,
    )
    return lane_hot, [row_iota == row[j : j + 1, :] for j in range(CHUNK)]


def pick(table, lane_hot, match, comps):
    tall, n = match[0].shape
    wide = jnp.dot(
        table, jnp.concatenate([lane_hot, lane_hot], axis=0), preferred_element_type=f32
    )
    out = []
    for c in range(comps):
        rows = []
        for j in range(CHUNK):
            block = wide[c * tall : (c + 1) * tall, j * n : (j + 1) * n]
            rows.append(jnp.sum(jnp.where(match[j], block, 0.0), axis=0, keepdims=True))
        out.append(jnp.concatenate(rows, axis=0))
    return out


def spread(values, lane_hot, match):
    blocks = []
    for v in values:
        for half in halves(v):
            half = half.astype(f32)
            blocks.append(
                jnp.concatenate(
                    [
                        jnp.where(match[j], half[j : j + 1, :], 0.0).astype(bf16)
                        for j in range(CHUNK)
                    ],
                    axis=1,
                )
            )
    return lax.dot_general(
        jnp.concatenate(blocks, axis=0),
        lane_hot,
        (((1,), (1,)), ((), ())),
        preferred_element_type=f32,
    )


def joined(halved, comps, tall):
    return [
        halved[2 * c * tall : (2 * c + 1) * tall] + halved[(2 * c + 1) * tall : (2 * c + 2) * tall]
        for c in range(comps)
    ]


def as_table(blocks):
    both = [halves(b) for b in blocks]
    return jnp.concatenate(
        [
            jnp.concatenate([b[0] for b in both], axis=0),
            jnp.concatenate([b[1] for b in both], axis=0),
        ],
        axis=1,
    )


def exact_dot(a, b):
    return jnp.dot(a, b, precision=lax.Precision.HIGHEST, preferred_element_type=f32)


def flat_block(u, c):
    return jnp.concatenate([u[c, i] for i in range(u.shape[1])], axis=0)


def slot_matrix(col, row, capacity, slots):
    pairs = row.shape[1]
    earlier = lax.broadcasted_iota(jnp.int32, (pairs, pairs), 0) < lax.broadcasted_iota(
        jnp.int32, (pairs, pairs), 1
    )
    rank = jnp.sum(jnp.where((col == row) & earlier, 1.0, 0.0), axis=0, keepdims=True)
    slot = row * capacity + rank.astype(jnp.int32)
    return jnp.where(
        lax.broadcasted_iota(jnp.int32, (slots, pairs), 0) == slot, 1.0, 0.0
    ).astype(f32)


def frames(u):
    span_x, span_y, lanes = u.shape[1:]
    iota_x = lax.broadcasted_iota(jnp.int32, (span_x, span_y, lanes), 0)
    iota_y = lax.broadcasted_iota(jnp.int32, (span_x, span_y, lanes), 1)
    valid = (iota_x < span_x - 1) & (iota_y < span_y - 1)

    def shift_x(v):
        return jnp.concatenate([v[1:], v[:1]], axis=0)

    def shift_y(v):
        return jnp.stack([pltpu.roll(v[i], span_y - 1, 0) for i in range(span_x)])

    one = [u[c] for c in range(3)]
    two = [shift_x(v) for v in one]
    four = [shift_y(v) for v in one]
    three = [shift_x(v) for v in four]
    centroid = [(one[c] + two[c] + three[c] + four[c]) * 0.25 for c in range(3)]
    a = [three[0] - one[0] + 1.0, three[1] - one[1] + 1.0, three[2] - one[2]]
    b = [four[0] - two[0] - 1.0, four[1] - two[1] + 1.0, four[2] - two[2]]
    normal = [
        a[1] * b[2] - a[2] * b[1],
        a[2] * b[0] - a[0] * b[2],
        a[0] * b[1] - a[1] * b[0],
    ]
    square = normal[0] * normal[0] + normal[1] * normal[1] + normal[2] * normal[2]
    usable = valid & (square > 0.0)
    scale = jnp.where(usable, 1.0 / jnp.sqrt(jnp.where(usable, square, 1.0)), 0.0)
    return centroid, [v * scale for v in normal]


def axis_low(shape, dim, span, start, total):
    iota = lax.broadcasted_iota(jnp.int32, shape, dim)
    size = shape[dim]
    low = jnp.where(iota == size - 1, -1, iota)
    inside = (iota < span) | (iota == size - 1)
    return inside & (low + start >= 0) & (low + start <= total - 2)


def next_z(v):
    return pltpu.roll(v, v.shape[1] - 1, 1)


def next_y(v):
    return pltpu.roll(v, v.shape[0] - 1, 0)


def plane_modes(plane):
    ahead = next_z(plane)
    total, diff = ahead + plane, ahead - plane
    total_y, diff_y = next_y(total), next_y(diff)
    return total_y + total, total_y - total, diff_y + diff, diff_y - diff


def fused_kernel(
    sizes,
    u_hbm, v_hbm, lame_hbm, shear_hbm, mass_hbm, slaves_hbm, gap_hbm, chosen_hbm, row_hbm,
    patch_hbm, faces_hbm,
    uo_ref, vo_ref,
    u_ref, v_ref, lame_ref, shear_ref, mass_ref, slaves_ref, gap_ref, chosen_ref, row_ref,
    patch_ref, faces_ref, load_sem,
    ring, z_in, y_out, y_in, elem, slot_ref, rows_ref, nodes_ref, halved_ref, inner_ref,
    fix_out, fix_in, out_1, out_2, in_1, in_2, force_1, force_2, back_1, back_2,
    fix_send, fix_recv, go_send, go_recv, back_send, back_recv, halo_send, halo_recv,
):
    n_len, n_wid, n_lay = sizes
    groups = n_len * n_wid
    span_x, span_y, span_z = u_ref.shape[1:]
    tall = span_x * span_y
    capacity, n = out_1.shape[2:]
    slots = groups * capacity
    per = CHUNK // capacity
    pairs = slaves_ref.shape[0]
    patches = faces_ref.shape[0]
    ring_y, ring_z = ring.shape[3:]
    blocks = groups // per
    side_by = 2 if blocks % 2 == 0 and pairs // CHUNK % 2 == 0 else 1
    at_len, at_wid, at_lay = lax.axis_index("len"), lax.axis_index("wid"), lax.axis_index("lay")
    me = at_len * n_wid + at_wid

    def peer_id(g):
        return (g // n_wid, g % n_wid, at_lay)

    loads = [
        pltpu.make_async_copy(src, dst, load_sem.at[i])
        for i, (src, dst) in enumerate(
            (
                (row_hbm, row_ref), (patch_hbm, patch_ref), (gap_hbm, gap_ref),
                (chosen_hbm, chosen_ref), (u_hbm, u_ref), (slaves_hbm, slaves_ref),
                (lame_hbm, lame_ref), (shear_hbm, shear_ref), (faces_hbm, faces_ref),
                (v_hbm, v_ref), (mass_hbm, mass_ref),
            )
        )
    ]
    for load in loads:
        load.start()

    zero_plane = jnp.zeros((ring_y, ring_z), f32)
    for s in range(STEPS):
        for c in range(5 if s == 0 else 3):
            for i in (span_x, span_x + 1):
                ring[s, c, i] = zero_plane

    barrier = pltpu.get_barrier_semaphore()

    def greet(o, _):
        pl.semaphore_signal(
            barrier, inc=1, device_id=peer_id((me + o) % groups), device_id_type=MESH
        )
        return 0

    lax.fori_loop(1, groups, greet, 0)
    lay_peers = [(at_lay + step) % n_lay for step in sorted({1 % n_lay, (n_lay - 1) % n_lay} - {0})]
    for other in lay_peers:
        pl.semaphore_signal(barrier, inc=1, device_id=(at_len, at_wid, other), device_id_type=MESH)
    pl.semaphore_wait(barrier, groups - 1 + len(lay_peers))
    for load in loads:
        load.wait()

    def halo_copy(s, phase, side):
        comps = pl.ds(0, 5 if s == 0 else 3)
        step = 1 if side == 0 else -1
        place = [at_len, at_wid, at_lay]
        axis = 2 - phase
        count = (n_len, n_wid, n_lay)[axis]
        place[axis] = place[axis] + step
        has = (place[axis] >= 0) & (place[axis] < count)
        if phase == 0:
            src = ring.at[s, comps, pl.ds(0, span_x), pl.ds(0, span_y), pl.ds(0, span_z)]
            dst = z_in.at[s, side, comps]
        elif phase == 1:
            src = y_out.at[s, side, comps]
            dst = y_in.at[s, side, comps]
        else:
            src = ring.at[s, comps, span_x - 1 if side == 0 else 0]
            dst = ring.at[s, comps, span_x + 1 if side == 0 else span_x]
        came = [at_len, at_wid, at_lay][axis] - step
        comes = (came >= 0) & (came < count)
        copy = pltpu.make_async_remote_copy(
            src_ref=src,
            dst_ref=dst,
            send_sem=halo_send.at[s, phase, side],
            recv_sem=halo_recv.at[s, phase, side],
            device_id=tuple(place),
            device_id_type=MESH,
        )
        return copy, has, comes

    def halo_start(s, phase):
        for side in range(2):
            copy, has, _ = halo_copy(s, phase, side)

            @pl.when(has)
            def _():
                copy.start()

    def halo_wait(s, phase):
        for side in range(2):
            copy, _, comes = halo_copy(s, phase, side)

            @pl.when(comes)
            def _():
                copy.wait_recv()

    def halo_sent(s):
        for phase in range(3):
            for side in range(2):
                copy, has, _ = halo_copy(s, phase, side)

                @pl.when(has)
                def _():
                    copy.wait_send()

    def fix_copy(g, slot):
        return pltpu.make_async_remote_copy(
            src_ref=fix_out.at[g],
            dst_ref=fix_in.at[slot],
            send_sem=fix_send.at[g],
            recv_sem=fix_recv.at[slot],
            device_id=peer_id(g),
            device_id_type=MESH,
        )

    def go_copy(s, g, slot):
        return pltpu.make_async_remote_copy(
            src_ref=(out_1, out_2)[s].at[g],
            dst_ref=(in_1, in_2)[s].at[slot],
            send_sem=go_send.at[s, g],
            recv_sem=go_recv.at[s, slot],
            device_id=peer_id(g),
            device_id_type=MESH,
        )

    def back_copy(s, g, slot):
        return pltpu.make_async_remote_copy(
            src_ref=(force_1, force_2)[s].at[g],
            dst_ref=(back_1, back_2)[s].at[slot],
            send_sem=back_send.at[s, g],
            recv_sem=back_recv.at[s, slot],
            device_id=peer_id(g),
            device_id_type=MESH,
        )

    def to_groups(rows):
        return rows.reshape(groups, capacity, n)

    def held(ref, b, c):
        return jnp.concatenate([ref[b * per + k, c] for k in range(per)], axis=0)

    faces = faces_ref[...]
    face_table = jnp.concatenate(
        [(faces // n).astype(f32).astype(bf16), (faces % n).astype(f32).astype(bf16)], axis=0
    )
    face_table = jnp.concatenate([face_table, jnp.zeros_like(face_table)], axis=1)
    lanes_z = lax.broadcasted_iota(jnp.int32, (span_y, span_z), 1)
    rows_y = lax.broadcasted_iota(jnp.int32, (ring_y - span_y, ring_z), 0)

    diagonal = lax.broadcasted_iota(jnp.int32, (pairs, pairs), 0) == lax.broadcasted_iota(
        jnp.int32, (pairs, pairs), 1
    )

    def column(row):
        return jnp.sum(jnp.where(diagonal, row.astype(f32), 0.0), axis=1, keepdims=True).astype(
            jnp.int32
        )

    row = row_ref[...]
    to_slot = slot_matrix(column(row), row, capacity, slots)
    slot_ref[...] = jnp.concatenate([to_slot, to_slot], axis=1).astype(bf16)
    face_id = (column(patch_ref[...]) * n + chosen_ref[...] + 1).astype(f32)
    fix_out[:, 0] = to_groups(exact_dot(to_slot, gap_ref[...]))
    fix_out[:, 1] = to_groups(exact_dot(to_slot, face_id) - 1.0)
    fix_in[me] = fix_out[me]

    for s in range(STEPS):
        comps = 5 if s == 0 else 3
        now_u, now_v = (u_ref, v_ref) if s == 0 else (uo_ref, vo_ref)
        out, into, force_ref, back = (
            (out_1, in_1, force_1, back_1) if s == 0 else (out_2, in_2, force_2, back_2)
        )
        for c in range(comps):
            for i in range(span_x):
                ring[s, c, i, 0:span_y, 0:span_z] = (
                    now_u[c, i] if c < 3 else (lame_ref, shear_ref)[c - 3][i]
                )
        halo_start(s, 0)
        if s == 0:

            def send_fix(o, _):
                fix_copy((me + o) % groups, me).start()
                return 0

            lax.fori_loop(1, groups, send_fix, 0)

        u = now_u[...]
        table = as_table([flat_block(u, c) for c in range(3)])

        to_slots = slot_ref[...]

        def gather_rows(t, _):
            for q in range(side_by):
                at = pl.ds(pl.multiple_of((t * side_by + q) * CHUNK, CHUNK), CHUNK)
                got = pick(table, *hots(slaves_ref[at, :], span_z, tall), 3)
                for c in range(3):
                    rows_ref[c, at, :] = got[c]
            return 0

        lax.fori_loop(0, pairs // CHUNK // side_by, gather_rows, 0)
        both = [halves(rows_ref[c]) for c in range(3)]
        moved = jnp.dot(
            to_slots,
            jnp.concatenate([jnp.concatenate([b[k] for b in both], axis=1) for k in range(2)], axis=0),
            preferred_element_type=f32,
        )
        for c in range(3):
            out[:, c] = to_groups(moved[:, c * n : (c + 1) * n])
        into[me] = out[me]

        def send_go(o, _):
            go_copy(s, (me + o) % groups, me).start()
            return 0

        lax.fori_loop(1, groups, send_go, 0)

        halo_wait(s, 0)
        for c in range(comps):
            for i in range(span_x):
                tile = jnp.where((lanes_z == 0) & (at_lay + 1 < n_lay), z_in[s, 1, c, i], 0.0)
                tile = jnp.where((lanes_z == span_z - 1) & (at_lay > 0), z_in[s, 0, c, i], tile)
                ring[s, c, i, 0:span_y, span_z:ring_z] = tile
        for c in range(comps):
            for i in range(span_x):
                y_out[s, 0, c, i : i + 1, :] = ring[s, c, i, span_y - 1 : span_y, :]
                y_out[s, 1, c, i : i + 1, :] = ring[s, c, i, 0:1, :]
        halo_start(s, 1)

        centroid, normal = frames(u)
        frame_table = as_table(
            [jnp.concatenate([v[i] for i in range(span_x)], axis=0) for v in centroid + normal]
        )
        halved_ref[...] = jnp.zeros_like(halved_ref)

        halo_wait(s, 1)
        for c in range(comps):
            for i in range(span_x):
                tile = jnp.where(
                    (rows_y == 0) & (at_wid + 1 < n_wid), y_in[s, 1, c, i : i + 1, :], 0.0
                )
                tile = jnp.where(
                    (rows_y == ring_y - span_y - 1) & (at_wid > 0), y_in[s, 0, c, i : i + 1, :], tile
                )
                ring[s, c, i, span_y:ring_y, :] = tile
        halo_start(s, 2)

        planes = [span_x + 1] + list(range(span_x + 1))
        shape = (ring_y, ring_z)

        def material(e):
            valid = axis_low(shape, 0, span_y, at_wid * span_y, n_wid * span_y) & axis_low(
                shape, 1, span_z, at_lay * span_z, n_lay * span_z
            )
            low = at_len * span_x + e - 1
            there = valid & (low >= 0) & (low <= n_len * span_x - 2)
            for m in range(2):
                sums = [plane_modes(ring[0, 3 + m, planes[e + k]])[0] for k in range(2)]
                elem[m, e] = jnp.where(there, (sums[0] + sums[1]) * 0.125, 0.0)

        def settle(i, modes):
            for c in range(3):
                none, y, z, yz = modes[c]
                even = pltpu.roll(none + z, 1, 1) + (none - z)
                odd = pltpu.roll(y + yz, 1, 1) + (y - yz)
                node = pltpu.roll(even + odd, 1, 0) + (even - odd)
                inner_ref[c, i] += node[0:span_y, 0:span_z]

        def internal(elements):
            carried, last = None, None
            for e in elements:
                if s == 0:
                    material(e)
                if e - 1 == last:
                    below = above
                else:
                    if carried is not None and last < span_x:
                        settle(last, carried)
                    carried = None
                    below = [plane_modes(ring[s, c, planes[e]]) for c in range(3)]
                above = [plane_modes(ring[s, c, planes[e + 1]]) for c in range(3)]
                lame, shear = elem[0, e], elem[1, e]
                grad = [
                    [
                        0.25 * (above[c][0] - below[c][0]),
                        0.25 * (above[c][1] + below[c][1]),
                        0.25 * (above[c][2] + below[c][2]),
                    ]
                    for c in range(3)
                ]
                pressure = lame * (grad[0][0] + grad[1][1] + grad[2][2])
                sheared = -0.25 * shear
                damped = (-0.125 * hourglass) * shear
                lower, upper = [], []
                for c in range(3):
                    lin = [sheared * (grad[c][j] + grad[j][c]) for j in range(3)]
                    lin[c] = lin[c] - 0.25 * pressure
                    h_xy = damped * (above[c][1] - below[c][1])
                    h_xz = damped * (above[c][2] - below[c][2])
                    h_yz = damped * (above[c][3] + below[c][3])
                    h_xyz = damped * (above[c][3] - below[c][3])
                    lower.append([-lin[0], lin[1] - h_xy, lin[2] - h_xz, h_yz - h_xyz])
                    upper.append([lin[0], lin[1] + h_xy, lin[2] + h_xz, h_yz + h_xyz])
                if e > 0:
                    if carried is None:
                        settle(e - 1, lower)
                    else:
                        settle(e - 1, [[p + q for p, q in zip(carried[c], lower[c])] for c in range(3)])
                carried, last = upper, e
            if last < span_x:
                settle(last, carried)

        inner_ref[...] = jnp.zeros_like(inner_ref)
        internal(list(range(1, span_x)))

        def landed(t):
            return [(me // per - t * side_by - q + 2 * blocks) % blocks for q in range(side_by)]

        def others(t, act):
            for b in landed(t):
                for k in range(per):
                    g = b * per + k

                    @pl.when(g != me)
                    def _():
                        act(g)

        if s == 0:

            def resolve(t, _):
                others(t, lambda g: fix_copy(g, g).wait_recv())
                for b in landed(t):
                    face_id = held(fix_in, b, 1).astype(jnp.int32)
                    high, low = pick(face_table, *hots(face_id, n, patches), 2)
                    node = high.astype(jnp.int32) * span_z + low.astype(jnp.int32)
                    nodes_ref[b] = jnp.where(face_id < 0, -1, node)
                return 0

            lax.fori_loop(0, blocks // side_by, resolve, 0)

        def own(t, _):
            others(t, lambda g: go_copy(s, g, g).wait_recv())
            added = []
            for b in landed(t):
                lane_hot, match = hots(nodes_ref[b], span_z, tall)
                got = pick(frame_table, lane_hot, match, 6)
                gap = held(fix_in, b, 0)
                for c in range(3):
                    gap = gap + (held(into, b, c) - got[c]) * got[3 + c]
                push = -penalty * jnp.minimum(gap, 0.0)
                force = [push * got[3 + c] for c in range(3)]
                for c in range(3):
                    for k in range(per):
                        force_ref[b * per + k, c] = force[c][k * capacity : (k + 1) * capacity]
                added.append(spread(force, lane_hot, match))
            others(t, lambda g: back_copy(s, g, me).start())
            halved_ref[...] += functools.reduce(jnp.add, added)
            return 0

        lax.fori_loop(0, blocks // side_by, own, 0)
        back[me] = force_ref[me]

        total = joined(halved_ref[...], 3, tall)
        zero = jnp.zeros((span_y, span_z), f32)
        for c in range(3):
            quarter = [-0.25 * total[c][i * span_y : (i + 1) * span_y] for i in range(span_x)]
            for i in range(span_x):
                both = (quarter[i] if i < span_x - 1 else zero) + (quarter[i - 1] if i else zero)
                inner_ref[c, i] += both + pltpu.roll(both, 1, 0)

        halo_wait(s, 2)
        internal([0, span_x])

        def wait_back(o, _):
            g = (me + o) % groups
            back_copy(s, g, g).wait_recv()
            return 0

        lax.fori_loop(1, groups, wait_back, 0)
        both = [halves(back[:, c].reshape(slots, n)) for c in range(3)]
        moved = lax.dot_general(
            to_slots[:, 0:pairs],
            jnp.concatenate([b[k] for k in range(2) for b in both], axis=1),
            (((0,), (0,)), ((), ())),
            preferred_element_type=f32,
        )
        for c in range(3):
            rows_ref[c] = moved[:, c * n : (c + 1) * n] + moved[:, (3 + c) * n : (4 + c) * n]
        halved_ref[...] = jnp.zeros_like(halved_ref)

        def scatter_rows(t, _):
            added = []
            for q in range(side_by):
                at = pl.ds(pl.multiple_of((t * side_by + q) * CHUNK, CHUNK), CHUNK)
                added.append(
                    spread(
                        [rows_ref[c, at, :] for c in range(3)],
                        *hots(slaves_ref[at, :], span_z, tall),
                    )
                )
            halved_ref[...] += functools.reduce(jnp.add, added)
            return 0

        lax.fori_loop(0, pairs // CHUNK // side_by, scatter_rows, 0)
        total = joined(halved_ref[...], 3, tall)
        for i in range(span_x):
            rate = time_step / mass_ref[i]
            for c in range(3):
                force = inner_ref[c, i] + total[c][i * span_y : (i + 1) * span_y]
                speed = now_v[c, i] + rate * force
                vo_ref[c, i] = speed
                uo_ref[c, i] = now_u[c, i] + time_step * speed

    for s in range(STEPS):
        halo_sent(s)

        def sent(o, _):
            g = (me + o) % groups
            if s == 0:
                fix_copy(g, me).wait_send()
            go_copy(s, g, me).wait_send()
            back_copy(s, g, me).wait_send()
            return 0

        lax.fori_loop(1, groups, sent, 0)


def per_device(
    displacement,
    velocity,
    lame_first,
    shear_modulus,
    nodal_mass,
    slave_nodes,
    initial_gap,
    candidate,
    pair_owner,
    pair_patch,
    master_faces,
):
    span_x, span_y, span_z = displacement.shape[1:]
    sizes = tuple(lax.axis_size(a) for a in ("len", "wid", "lay"))
    groups = sizes[0] * sizes[1]
    pairs, n = slave_nodes.shape[3:]
    patches = master_faces.shape[3]
    capacity = max(2, 2 * pairs // groups)
    slots = groups * capacity
    tall = span_x * span_y
    ring_y, ring_z = span_y + 8, span_z + 128
    args = (
        displacement,
        velocity,
        lame_first,
        shear_modulus,
        nodal_mass,
        slave_nodes.reshape(pairs, n),
        initial_gap.reshape(pairs, n),
        candidate.reshape(pairs, n),
        pair_owner.reshape(1, pairs),
        pair_patch.reshape(1, pairs),
        master_faces.reshape(patches, n),
    )
    block = (3, span_x, span_y, span_z)
    vm = lambda *shape: pltpu.VMEM(shape, f32)
    fixed, slim = (groups, 2, capacity, n), (groups, 3, capacity, n)
    dma = lambda *shape: pltpu.SemaphoreType.DMA(shape)
    return pl.pallas_call(
        functools.partial(fused_kernel, sizes),
        out_shape=[jax.ShapeDtypeStruct(block, f32)] * 2,
        in_specs=[pl.BlockSpec(memory_space=pltpu.HBM)] * len(args),
        out_specs=[pl.BlockSpec(memory_space=pltpu.VMEM)] * 2,
        scratch_shapes=[
            *[pltpu.VMEM(a.shape, a.dtype) for a in args],
            dma(len(args)),
            vm(STEPS, 5, span_x + 2, ring_y, ring_z),
            vm(STEPS, 2, 5, span_x, span_y, span_z),
            vm(STEPS, 2, 5, span_x, ring_z),
            vm(STEPS, 2, 5, span_x, ring_z),
            vm(2, span_x + 1, ring_y, ring_z),
            pltpu.VMEM((slots, 2 * pairs), bf16),
            vm(3, pairs, n),
            pltpu.VMEM((slots // CHUNK, CHUNK, n), jnp.int32),
            vm(6 * tall, span_z),
            vm(*block),
            vm(*fixed), vm(*fixed), vm(*slim), vm(*slim), vm(*slim), vm(*slim),
            vm(*slim), vm(*slim), vm(*slim), vm(*slim),
            dma(groups), dma(groups),
            dma(STEPS, groups), dma(STEPS, groups), dma(STEPS, groups), dma(STEPS, groups),
            dma(STEPS, 3, 2), dma(STEPS, 3, 2),
        ],
        compiler_params=pltpu.CompilerParams(
            collective_id=0, has_side_effects=True, vmem_limit_bytes=64 * 1024 * 1024
        ),
    )(*args)


def solution(mesh):
    in_specs = (
        P(None, "len", "wid", "lay"),
        P(None, "len", "wid", "lay"),
        P("len", "wid", "lay"),
        P("len", "wid", "lay"),
        P("len", "wid", "lay"),
        P("len", "wid", "lay", None, None),
        P("len", "wid", "lay", None, None),
        P("len", "wid", "lay", None, None),
        P("len", "wid", "lay", None, None),
        P("len", "wid", "lay", None),
        P("len", "wid", "lay", None, None),
    )
    out_specs = (P(None, "len", "wid", "lay"), P(None, "len", "wid", "lay"))
    return jax.shard_map(
        per_device, mesh=mesh, in_specs=in_specs, out_specs=out_specs, check_vma=False
    )
```
